32 devices in a mesh: groups: 2 (over y), expert: 4 (over z), tensor: 4 (over x, core).
Axes of the slice: x: 2, y: 2, z: 4, core: 2. Of those that a mesh axis runs over, the one named last changes fastest.
Arguments:
- resid: bfloat16 [256, 3072], P(('groups', 'expert', 'tensor')), parts along dimension 0, may hold values from -6 to 6
- attn_part: bfloat16 [256, 12288], P(('groups', 'expert'), 'tensor'), parts along dimension 0, may hold values from -2 to 2
- norm_gain: float32 [3072], replicated, may hold values from 0.1 to 1.9
- w_router: bfloat16 [3072, 8], replicated, may hold values from -0.3125 to 0.3125
- routes: int32 [256, 2], P(('groups', 'expert', 'tensor')), parts along dimension 0, may hold values from 0 to 7, all different within a row; in each aligned block of 8 rows (0 to 7, 8 to 15, ...) at most 4 rows name the same one
- w_gate: bfloat16 [3072, 65536], P(None, ('expert', 'tensor')), may hold values from -0.109375 to 0.109375
- w_up: bfloat16 [3072, 65536], P(None, ('expert', 'tensor')), may hold values from -0.109375 to 0.109375
- w_down: bfloat16 [65536, 3072], P(('expert', 'tensor')), may hold values from -0.0625 to 0.0625
Outputs:
- block_out: bfloat16 [256, 3072], P(('groups', 'expert', 'tensor')), parts along dimension 0
The draws below stay inside these ranges and needn't reach their ends.
There are 2 independent parts, one for each index of `groups`. The reference program is written for one: setup_inputs(seed, part) draws one part's arguments, and reference() takes and returns one part's arrays. A program takes and returns all parts, laid end to end along the dimension named above; an argument that names none is the same for every part. Nothing has to cross between parts.
Inputs may be any that keep to these rules, and one draw needn't show every extreme that they name: `routes`: the two entries of a row differ. Within the 8 rows of one device no expert is named more than 4 times, and in some device's rows some expert is named exactly 4 times.
All inputs are finite; a program needn't handle non-finite values.
Results may differ from the reference program's by a relative error of at most 0.02.
Values may be sent and summed in bfloat16 or wider, within the bound.
A program may use at most 128 MiB of HBM per device.

```python
import math
import jax
import jax.numpy as jnp
import numpy as np
from jax import lax

D = 3072
FF = 8192
E = 8
TOK_DEV = 8
CAP = 4
TOKENS = 128
N_TENSOR = 4


def block_levels(key, dims, split, least, top_value):
    level, own = 1.0, jax.random.fold_in(key, 6)
    for dim, shards_of in split:
        draws = jnp.exp(jax.random.uniform(jax.random.fold_in(own, dim), (shards_of,), jnp.float32, least / len(split), top_value / len(split)))
        level = level * jnp.repeat(draws, dims[dim] // shards_of).reshape([-1 if axis == dim else 1 for axis in range(len(dims))])
    return level


def shared_out(rng, own, number, rows, amount, top, most, slope):
    sequence = jax.random.permutation(rng, amount)
    heavy_load, usual = load_shares(amount, rows * top, most, slope, True), load_shares(amount, rows * top, most, slope, False)
    places = jnp.arange(amount)

    def named(sizes, offset_by):
        used = int((sizes > 0).sum())
        fixed = max(1, used // 4)
        shifted = fixed + (places - fixed + offset_by * (used - fixed)) % max(1, amount - fixed)
        return jnp.zeros((amount,), jnp.int32).at[sequence[jnp.where(places < fixed, places, shifted)]].set(jnp.asarray(sizes, jnp.int32))

    sizes = jnp.where(number % 4 == 0, named(heavy_load, number // 4), named(usual, number - number // 4 - 1))
    mixed = jax.random.permutation(jax.random.fold_in(own, 3), amount)
    source_of, taker = mixed[0:amount // 2 * 2:2], mixed[1:amount // 2 * 2:2]
    slack = jnp.minimum(sizes[source_of] - 1, most - sizes[taker]) // 2
    slack = jnp.where((source_of == sequence[0]) | (taker == sequence[0]) | (sizes[taker] == 0), 0, jnp.maximum(slack, 0))
    shifted = jax.random.randint(jax.random.fold_in(own, 4), (amount // 2,), 0, 1 << 20) % (slack + 1)
    sizes = sizes.at[source_of].add(-shifted).at[taker].add(shifted)
    members = jnp.searchsorted(jnp.cumsum(sizes), jnp.arange(rows * top), side="right").astype(jnp.int32)
    listing = members.reshape(top, rows).T
    listing = listing[jax.random.permutation(jax.random.fold_in(own, 1), rows)]
    offset_by = jax.random.randint(jax.random.fold_in(own, 2), (rows, 1), 0, top)
    return jnp.take_along_axis(listing, (jnp.arange(top)[None, :] + offset_by) % top, axis=1)


def load_shares(amount, total, limit, skew, full):
    loads = [(1 << 20) // math.isqrt(standing ** skew) + 1 for standing in range(1, amount + 1)]
    largest = limit if full else min(limit, max(-(-total // amount), total * loads[0] // sum(loads)))
    least = 1 if total - largest >= amount - 1 else 0
    holding, spare = [largest] + [least] * (amount - 1), total - largest - least * (amount - 1)
    while spare > 0:
        movable = [i for i in range(1, amount) if holding[i] < largest] or [i for i in range(1, amount) if holding[i] < limit]
        whole, remaining = sum([loads[i] for i in movable]), spare
        for i in movable:
            more = min(limit - holding[i], max(1, remaining * loads[i] // whole), spare)
            holding[i] = holding[i] + more
            spare = spare - more
    return np.array(holding)


def normal_values(rng, shape, scale, most, shards=(), kind=jnp.bfloat16):
    loudness = block_levels(rng, shape, shards, -0.22, 0.18) if shards else 1.0
    drawn = jax.random.normal(rng, shape, jnp.float32) * scale * loudness
    return jnp.minimum(jnp.maximum(drawn, -most), most).astype(kind)


def setup_inputs(seed: int = 0, part: int = 0) -> dict:
    keys = jax.random.split(jax.random.key(seed), 9)
    part_keys = jax.random.split(jax.random.fold_in(keys[8], part), 9)
    resid = normal_values(part_keys[0], (TOKENS, D), 1.0, 6.0, ((0, 16),))
    attn_part = normal_values(part_keys[1], (TOKENS, N_TENSOR * D), 0.35, 2.0, ((0, 4), (1, 4)))
    norm_gain = jnp.clip(1.0 + 0.18 * jax.random.normal(keys[2], (D,), jnp.float32), 0.1, 1.9)
    w_router = normal_values(keys[3], (D, E), (D // 8) ** -0.5, 0.3125)
    routes_keys = jax.random.split(jax.random.fold_in(part_keys[4], 1), TOKENS // TOK_DEV)
    routes_turns = jax.random.permutation(jax.random.fold_in(part_keys[4], 3), TOKENS // TOK_DEV)
    routes = jax.vmap(lambda own, number: shared_out(jax.random.fold_in(part_keys[4], 2), own, number, TOK_DEV, E, 2, CAP, 2))(routes_keys, routes_turns).reshape((TOKENS, 2))
    w_gate = normal_values(keys[5], (D, E * FF), D ** -0.5, 0.109375, ((1, 16),))
    w_up = normal_values(keys[6], (D, E * FF), D ** -0.5, 0.109375, ((1, 16),))
    w_down = normal_values(keys[7], (E * FF, D), FF ** -0.5, 0.0625, ((0, 16),))
    return dict(resid=resid, attn_part=attn_part, norm_gain=norm_gain, w_router=w_router, routes=routes, w_gate=w_gate, w_up=w_up, w_down=w_down)


EPSILON = 1e-05

def reference(resid, attn_part, norm_gain, w_router, routes, w_gate, w_up, w_down):
    token_count = resid.shape[0]
    attn_sum = lax.optimization_barrier(jnp.sum(attn_part.astype(jnp.float32).reshape(token_count, N_TENSOR, D), axis=1))
    hidden_state = (resid.astype(jnp.float32) + attn_sum).astype(jnp.bfloat16)
    hidden_wide = lax.optimization_barrier(hidden_state).astype(jnp.float32)
    inverse_rms = lax.rsqrt(lax.optimization_barrier(jnp.mean(hidden_wide * hidden_wide, axis=1, keepdims=True)) + EPSILON)
    normed = (hidden_wide * inverse_rms * norm_gain.astype(jnp.float32)).astype(jnp.bfloat16)
    logits = jnp.dot(normed, w_router, preferred_element_type=jnp.float32)
    first_logit = jnp.take_along_axis(logits, routes[:, 0:1], axis=1)[:, 0]
    second_logit = jnp.take_along_axis(logits, routes[:, 1:2], axis=1)[:, 0]
    share_first = jax.nn.sigmoid(first_logit - second_logit)
    share_second = 1.0 - share_first
    expert_range = jnp.arange(E, dtype=jnp.int32)
    per_token = lax.optimization_barrier(jnp.sum((routes[:, :, None] == expert_range).astype(jnp.int32), axis=1))
    block_count = token_count // TOK_DEV
    blocked = per_token.reshape(block_count, TOK_DEV, E)
    running = (jnp.cumsum(blocked, axis=1) - blocked).reshape(token_count, E).astype(jnp.int32)
    block_index = jnp.arange(token_count, dtype=jnp.int32) // TOK_DEV
    column_count = block_count * CAP
    targets = []
    for pick_index in range(2):
        chosen = routes[:, pick_index]
        slot_index = jnp.take_along_axis(running, routes[:, pick_index:pick_index + 1], axis=1)[:, 0]
        targets.append((chosen * column_count + block_index * CAP + slot_index).astype(jnp.int32))
    expert_input = jnp.zeros((E * column_count, D), jnp.bfloat16)
    expert_input = expert_input.at[targets[0]].set(normed).at[targets[1]].set(normed)
    expert_input = expert_input.reshape(E, column_count, D)

    def run_expert(operands):
        expert_id, inputs = operands
        gate_cols = lax.dynamic_slice_in_dim(w_gate, expert_id * FF, FF, 1)
        up_cols = lax.dynamic_slice_in_dim(w_up, expert_id * FF, FF, 1)
        down_rows = lax.dynamic_slice_in_dim(w_down, expert_id * FF, FF, 0)
        gate_value = jnp.dot(inputs, gate_cols, preferred_element_type=jnp.float32)
        up_value = jnp.dot(inputs, up_cols, preferred_element_type=jnp.float32)
        activated = (jax.nn.silu(gate_value) * up_value).astype(jnp.bfloat16)
        return jnp.dot(activated, down_rows, preferred_element_type=jnp.float32)
    expert_output = lax.map(run_expert, (expert_range, expert_input)).reshape(E * column_count, D)
    mixed = hidden_wide + share_first[:, None] * expert_output[targets[0]] + share_second[:, None] * expert_output[targets[1]]
    return mixed.astype(jnp.bfloat16)
```

```python
import functools

import jax
import jax.numpy as jnp
from jax import lax
from jax.experimental import pallas as pl
from jax.experimental.pallas import tpu as pltpu
from jax.sharding import PartitionSpec as P

E = 8
MESH = pl.DeviceIdType.MESH


EPSILON = 1e-05


def partner(shard, axis, distance):
    return lax.ppermute(shard, axis, [(i, i ^ 1 << distance) for i in range(lax.axis_size(axis))])


def shards(resid, attn_part, norm_gain, w_router, routes, w_gate, w_up, w_down):
    expert_ranks = lax.axis_size("expert")
    tensor_ranks = lax.axis_size("tensor")
    my_expert_rank = lax.axis_index("expert")
    my_tensor_rank = lax.axis_index("tensor")
    token_rows = resid.shape[0]
    feature_count = resid.shape[1]
    holders = max(1, expert_ranks // E)
    hosted = max(1, E // expert_ranks)
    expert_groups = E // hosted
    capacity = token_rows // 2
    rank_slots = hosted * capacity
    feature_share = feature_count // holders
    levels = holders.bit_length() - 1
    partial_terms = attn_part.astype(jnp.float32)
    attn_rows = lax.psum_scatter(
        partial_terms.astype(jnp.bfloat16), "tensor", scatter_dimension=0, tiled=True
    ).astype(jnp.float32)
    hidden_state = (resid.astype(jnp.float32) + attn_rows).astype(jnp.bfloat16)
    hidden_wide = lax.optimization_barrier(hidden_state).astype(jnp.float32)
    inverse_rms = lax.rsqrt(jnp.mean(hidden_wide * hidden_wide, axis=1, keepdims=True) + EPSILON)
    normed = (hidden_wide * inverse_rms * norm_gain).astype(jnp.bfloat16)
    logits = jnp.dot(normed, w_router, preferred_element_type=jnp.float32)
    expert_columns = lax.broadcasted_iota(jnp.int32, (token_rows, E), 1)
    pick_first = (routes[:, 0:1] == expert_columns).astype(jnp.float32)
    pick_second = (routes[:, 1:2] == expert_columns).astype(jnp.float32)
    share_first = jax.nn.sigmoid(jnp.sum((pick_first - pick_second) * logits, axis=1))
    share_second = 1.0 - share_first
    row_later = lax.broadcasted_iota(jnp.int32, (token_rows, token_rows), 0)
    row_earlier = lax.broadcasted_iota(jnp.int32, (token_rows, token_rows), 1)
    earlier = (row_later > row_earlier).astype(jnp.float32)
    before = jnp.dot(earlier, pick_first + pick_second, precision=lax.Precision.HIGHEST)
    slot_first = jnp.sum(before * pick_first, axis=1)
    slot_second = jnp.sum(before * pick_second, axis=1)
    slot_numbers = lax.broadcasted_iota(jnp.int32, (token_rows, E, capacity), 2).astype(jnp.float32)
    cell_first = pick_first[:, :, None] * (slot_numbers == slot_first[:, None, None]).astype(
        jnp.float32
    )
    cell_second = pick_second[:, :, None] * (slot_numbers == slot_second[:, None, None]).astype(
        jnp.float32
    )
    placement = (
        (cell_first + cell_second)
        .reshape(token_rows, expert_groups, rank_slots)
        .astype(jnp.bfloat16)
    )
    combine_weight = (
        share_first[:, None, None] * cell_first + share_second[:, None, None] * cell_second
    ).reshape(token_rows, expert_groups, rank_slots)
    outgoing = jnp.einsum(
        "rgc,rd->gcd", placement, normed, preferred_element_type=jnp.float32
    ).astype(jnp.bfloat16)
    outgoing = jnp.repeat(outgoing, holders, axis=0)
    arrived = lax.all_to_all(outgoing, "expert", split_axis=0, concat_axis=0, tiled=True)
    device_span = my_expert_rank * tensor_ranks + my_tensor_rank
    own_expert = device_span * E // (expert_ranks * tensor_ranks)
    local_index = own_expert - my_expert_rank // holders * hosted

    def activate(token_block):
        source_count = token_block.shape[0]
        selected = lax.dynamic_slice_in_dim(token_block, local_index * capacity, capacity, 1)
        flattened = selected.reshape(source_count * capacity, feature_count)
        gate_value = jnp.dot(flattened, w_gate, preferred_element_type=jnp.float32)
        up_value = jnp.dot(flattened, w_up, preferred_element_type=jnp.float32)
        return (jax.nn.silu(gate_value) * up_value).astype(jnp.bfloat16)

    def expert_partial(token_block):
        source_count = token_block.shape[0]
        activated = activate(token_block)
        produced = jnp.dot(activated, w_down, preferred_element_type=jnp.float32).reshape(
            source_count, capacity, feature_count
        )
        if hosted == 1:
            return produced
        blank = jnp.zeros((source_count, rank_slots, feature_count), jnp.float32)
        return lax.dynamic_update_slice_in_dim(blank, produced, local_index * capacity, 1)

    partial_value = expert_partial(lax.all_gather(arrived, "tensor", axis=0, tiled=True))
    leading = partial_value.shape[0]
    layered = partial_value.reshape((leading, rank_slots) + (2,) * levels + (feature_share,))
    remaining = [section for section in range(levels - 1, -1, -1)]
    for section in range(levels):
        split_axis = 2 + remaining.index(section)
        my_side = my_expert_rank // 2**section % 2
        kept_half = lax.dynamic_index_in_dim(layered, my_side, split_axis, keepdims=False)
        given_half = lax.dynamic_index_in_dim(layered, 1 - my_side, split_axis, keepdims=False)
        layered = kept_half + partner(given_half.astype(jnp.bfloat16), "expert", section).astype(
            given_half.dtype
        )
        remaining = [other for other in remaining if other != section]
    own_sources = lax.psum_scatter(
        layered.astype(jnp.bfloat16), "tensor", scatter_dimension=0, tiled=True
    ).astype(jnp.float32)
    returned = lax.all_to_all(
        own_sources.astype(jnp.bfloat16), "expert", split_axis=0, concat_axis=0, tiled=True
    ).astype(own_sources.dtype)
    returned_view = returned.reshape(expert_groups, holders, rank_slots, feature_share)
    mixed = jnp.einsum(
        "rgc,gscp->rsp", combine_weight, returned_view, precision=lax.Precision.HIGHEST
    )
    mixed = mixed.reshape(token_rows, feature_count)
    return (hidden_wide + mixed).astype(jnp.bfloat16)


LANES = 128
PACKED_ROWS = 16
WEIGHT_BYTES = 52 << 20
VMEM_BYTES = 60 << 20


def fused_kernel(
    sizes,
    resid_hbm,
    attn_hbm,
    gain_hbm,
    router_hbm,
    routes_hbm,
    gate_hbm,
    up_hbm,
    down_hbm,
    out_ref,
    resid,
    attn,
    gain,
    router,
    routes,
    in_sem,
    hidden_weights,
    hidden_sem,
    down_weights,
    down_sem,
    attn_out,
    attn_in,
    attn_out_sem,
    attn_in_sem,
    hidden_ref,
    share_ref,
    slots_out,
    slots_in,
    slots_out_sem,
    slots_in_sem,
    pass_out_sem,
    pass_in_sem,
    tokens,
    activated,
    partial_ref,
    half_out,
    half_in,
    half_out_sem,
    half_in_sem,
    back_out,
    back_in,
    back_out_sem,
    back_in_sem,
):
    experts, tensor_ranks, capacity, hidden_slots, down_slots = sizes
    rows, features = resid.shape
    fold = PACKED_ROWS // capacity
    width = features // fold
    hidden_step = hidden_weights.shape[3]
    hidden_steps = gate_hbm.shape[1] // hidden_step
    down_step = down_weights.shape[2]
    down_steps = features // down_step
    pairs = tensor_ranks // 2
    group = lax.axis_index("groups")
    my_z = lax.axis_index("expert")
    my_t = lax.axis_index("tensor")
    core = my_t % 2
    me = my_z * pairs + my_t // 2
    sibling = (group, my_z, my_t + 1 - 2 * core)

    def holder(number):
        return (group, number // pairs, (number % pairs) * 2 + core)

    def after(step):
        return (me + step) % experts

    def before(step):
        return (me + experts - step) % experts

    small = [
        pltpu.make_async_copy(source, target, in_sem.at[i])
        for i, (source, target) in enumerate(
            (
                (attn_hbm, attn),
                (resid_hbm, resid),
                (gain_hbm, gain),
                (router_hbm, router),
                (routes_hbm, routes),
            )
        )
    ]
    for copy in small:
        copy.start()

    def hidden_copies(step, slot):
        columns = pl.ds(pl.multiple_of(step * hidden_step, hidden_step), hidden_step)
        return [
            pltpu.make_async_copy(
                source.at[:, columns], hidden_weights.at[slot, i], hidden_sem.at[slot, i]
            )
            for i, source in enumerate((gate_hbm, up_hbm))
        ]

    def down_copy(step, slot):
        columns = pl.ds(pl.multiple_of(step * down_step, down_step), down_step)
        return pltpu.make_async_copy(
            down_hbm.at[:, columns], down_weights.at[slot], down_sem.at[slot]
        )

    for step in range(hidden_slots):
        for copy in hidden_copies(step, step):
            copy.start()

    barrier = pltpu.get_barrier_semaphore()
    tensor_peers = [(group, my_z, (my_t + i) % tensor_ranks) for i in range(1, tensor_ranks)]
    peers = [holder(after(i)) for i in range(1, experts)]
    for peer in tensor_peers + peers:
        pl.semaphore_signal(barrier, inc=1, device_id=peer, device_id_type=MESH)

    small[0].wait()
    terms = attn[...].astype(jnp.float32)
    half = features // 2
    for i in range(tensor_ranks):
        block = terms[i * rows : (i + 1) * rows]
        attn_out[i] = jnp.concatenate([block[:, :half], block[:, half:]], axis=0).astype(
            jnp.bfloat16
        )
    pl.semaphore_wait(barrier, len(tensor_peers) + len(peers))

    def attn_copy(step):
        target = (my_t + step) % tensor_ranks
        return pltpu.make_async_remote_copy(
            src_ref=attn_out.at[target],
            dst_ref=attn_in.at[step - 1],
            send_sem=attn_out_sem.at[step - 1],
            recv_sem=attn_in_sem.at[step - 1],
            device_id=(group, my_z, target),
            device_id_type=MESH,
        )

    attn_copies = [attn_copy(step) for step in range(1, tensor_ranks)]
    for copy in attn_copies:
        copy.start()
    for copy in small[1:]:
        copy.wait()
    route = routes[...]
    first, second = route[:, 0:1], route[:, 1:2]
    columns = lax.broadcasted_iota(jnp.int32, (rows, LANES), 1)
    row_number = lax.broadcasted_iota(jnp.int32, (rows, LANES), 0)
    pick_first = (columns == first).astype(jnp.float32)
    pick_second = (columns == second).astype(jnp.float32)
    both = pick_first + pick_second
    earlier = jnp.zeros((rows, LANES), jnp.float32)
    for i in range(rows):
        earlier += jnp.where(row_number > i, both[i : i + 1], 0.0)
    slot_first = jnp.sum(earlier * pick_first, axis=1, keepdims=True).astype(jnp.int32)
    slot_second = jnp.sum(earlier * pick_second, axis=1, keepdims=True).astype(jnp.int32)
    place_first = jnp.concatenate([first * PACKED_ROWS + slot_first] * fold, axis=0)
    place_second = jnp.concatenate([second * PACKED_ROWS + slot_second] * fold, axis=0)
    packed = experts * PACKED_ROWS
    part = lax.broadcasted_iota(jnp.int32, (fold * rows, packed), 0) // rows * capacity
    cells = lax.broadcasted_iota(jnp.int32, (fold * rows, packed), 1) - part
    cell_first = (cells == place_first).astype(jnp.float32)
    cell_second = (cells == place_second).astype(jnp.float32)
    placement = (cell_first + cell_second).T.astype(jnp.bfloat16)

    summed = attn_out[my_t].astype(jnp.float32)
    for i, copy in enumerate(attn_copies):
        copy.wait_recv()
        summed += attn_in[i].astype(jnp.float32)
    attn_sum = jnp.concatenate([summed[:rows], summed[rows:]], axis=1)
    hidden_wide = (
        (resid[...].astype(jnp.float32) + attn_sum).astype(jnp.bfloat16).astype(jnp.float32)
    )
    hidden_ref[...] = hidden_wide
    mean_square = jnp.sum(hidden_wide * hidden_wide, axis=1, keepdims=True) / features
    normed_wide = hidden_wide * lax.rsqrt(mean_square + EPSILON) * gain[...]
    normed = normed_wide.astype(jnp.bfloat16)
    folded = jnp.concatenate(
        [normed_wide[:, i * width : (i + 1) * width] for i in range(fold)], axis=0
    ).astype(jnp.bfloat16)
    outgoing = jnp.dot(placement, folded, preferred_element_type=jnp.float32)
    slots_out[...] = outgoing.astype(jnp.bfloat16).reshape(experts, PACKED_ROWS, width)

    def slot_copy(step):
        return pltpu.make_async_remote_copy(
            src_ref=slots_out.at[after(step)],
            dst_ref=slots_in.at[core, me],
            send_sem=slots_out_sem.at[step],
            recv_sem=slots_in_sem.at[step],
            device_id=holder(after(step)),
            device_id_type=MESH,
        )

    def pass_copy(step):
        source = slots_out.at[me] if step == 0 else slots_in.at[core, before(step)]
        return pltpu.make_async_remote_copy(
            src_ref=source,
            dst_ref=slots_in.at[core, before(step)],
            send_sem=pass_out_sem.at[step],
            recv_sem=pass_in_sem.at[step],
            device_id=sibling,
            device_id_type=MESH,
        )

    slot_copies = [slot_copy(step) for step in range(1, experts)]
    for copy in slot_copies:
        copy.start()
    pass_copies = [pass_copy(step) for step in range(experts)]
    pass_copies[0].start()
    for step in range(down_slots):
        down_copy(step, step).start()
    slots_in[core, me] = slots_out[me]

    logits = jnp.dot(normed, router[...], preferred_element_type=jnp.float32)
    expert_columns = lax.broadcasted_iota(jnp.int32, (rows, experts), 1)
    logit_first = jnp.sum(jnp.where(expert_columns == first, logits, 0.0), axis=1, keepdims=True)
    logit_second = jnp.sum(jnp.where(expert_columns == second, logits, 0.0), axis=1, keepdims=True)
    share_first = 1.0 / (1.0 + jnp.exp(logit_second - logit_first))
    share_second = 1.0 - share_first
    share_ref[...] = (
        jnp.concatenate([share_first] * fold, axis=0) * cell_first
        + jnp.concatenate([share_second] * fold, axis=0) * cell_second
    )

    for step in range(1, experts):
        slot_copies[step - 1].wait_recv()
        pass_copies[step].start()
    for copy in pass_copies:
        copy.wait_recv()

    sources = 2 * experts
    token_rows = sources * capacity
    arrived = slots_in[...].reshape(sources * PACKED_ROWS, width)
    token_number = lax.broadcasted_iota(jnp.int32, (token_rows, sources * PACKED_ROWS), 0)
    packed_number = lax.broadcasted_iota(jnp.int32, (token_rows, sources * PACKED_ROWS), 1)
    wanted = token_number // capacity * PACKED_ROWS + token_number % capacity
    for i in range(fold):
        select = (packed_number == wanted + i * capacity).astype(jnp.float32).astype(jnp.bfloat16)
        tokens[:, i * width : (i + 1) * width] = jnp.dot(
            select, arrived, preferred_element_type=jnp.float32
        ).astype(jnp.bfloat16)

    def hidden_body(step, carry):
        slot = step % hidden_slots
        for copy in hidden_copies(step, slot):
            copy.wait()
        gate_value = jnp.dot(
            tokens[...], hidden_weights[slot, 0], preferred_element_type=jnp.float32
        )
        up_value = jnp.dot(tokens[...], hidden_weights[slot, 1], preferred_element_type=jnp.float32)
        value = gate_value / (1.0 + jnp.exp(-gate_value)) * up_value
        activated[:, pl.ds(pl.multiple_of(step * hidden_step, hidden_step), hidden_step)] = (
            value.astype(jnp.bfloat16)
        )

        @pl.when(step + hidden_slots < hidden_steps)
        def _():
            for copy in hidden_copies(step + hidden_slots, slot):
                copy.start()

        return carry

    lax.fori_loop(0, hidden_steps, hidden_body, 0)

    half_rows = experts * capacity

    def half_copy(step):
        return pltpu.make_async_remote_copy(
            src_ref=half_out.at[step],
            dst_ref=half_in.at[step],
            send_sem=half_out_sem.at[step],
            recv_sem=half_in_sem.at[step],
            device_id=sibling,
            device_id_type=MESH,
        )

    def back_copy(step, distance):
        return pltpu.make_async_remote_copy(
            src_ref=back_out.at[step, after(distance)],
            dst_ref=back_in.at[step, me],
            send_sem=back_out_sem.at[step, distance],
            recv_sem=back_in_sem.at[step, distance],
            device_id=holder(after(distance)),
            device_id_type=MESH,
        )

    to_row = lax.broadcasted_iota(jnp.int32, (packed, packed), 0)
    from_row = lax.broadcasted_iota(jnp.int32, (packed, packed), 1)
    origin = (
        to_row % PACKED_ROWS // capacity * half_rows
        + to_row // PACKED_ROWS * capacity
        + to_row % capacity
    )
    reorder = (from_row == origin).astype(jnp.float32).astype(jnp.bfloat16)

    def send_back(step):
        half_copy(step).wait_recv()
        total = partial_ref[step, core] + half_in[step].astype(jnp.float32)
        stacked = jnp.concatenate(
            [total[:, i * LANES : (i + 1) * LANES] for i in range(fold)], axis=0
        ).astype(jnp.bfloat16)
        ordered = jnp.dot(reorder, stacked, preferred_element_type=jnp.float32)
        back_out[step] = ordered.astype(jnp.bfloat16).reshape(experts, PACKED_ROWS, LANES)
        for distance in range(1, experts):
            back_copy(step, distance).start()
        back_in[step, me] = back_out[step, me]

    def down_body(step, carry):
        slot = step % down_slots
        down_copy(step, slot).wait()
        produced = jnp.dot(activated[...], down_weights[slot], preferred_element_type=jnp.float32)
        partial_ref[step] = produced.reshape(2, half_rows, down_step)

        @pl.when(step + down_slots < down_steps)
        def _():
            down_copy(step + down_slots, slot).start()

        half_out[step] = partial_ref[step, 1 - core].astype(jnp.bfloat16)
        half_copy(step).start()

        @pl.when(step > 0)
        def _():
            send_back(step - 1)

        return carry

    lax.fori_loop(0, down_steps, down_body, 0)
    send_back(down_steps - 1)

    for step in range(down_steps):
        for distance in range(1, experts):
            back_copy(step, distance).wait_recv()
        mixed = jnp.dot(
            share_ref[...],
            back_in[step].reshape(packed, LANES).astype(jnp.float32),
            precision=lax.Precision.HIGHEST,
            preferred_element_type=jnp.float32,
        )
        for i in range(fold):
            span = slice(step * down_step + i * LANES, step * down_step + (i + 1) * LANES)
            out_ref[:, span] = (
                hidden_ref[:, span] + mixed[i * rows : (i + 1) * rows]
            ).astype(jnp.bfloat16)

    for copy in attn_copies + slot_copies + pass_copies:
        copy.wait_send()
    for step in range(down_steps):
        half_copy(step).wait_send()
        for distance in range(1, experts):
            back_copy(step, distance).wait_send()


def fused_shards(resid, attn_part, norm_gain, w_router, routes, w_gate, w_up, w_down):
    tensor_ranks = lax.axis_size("tensor")
    rows, features = resid.shape
    capacity = rows // 2
    fold = PACKED_ROWS // capacity
    width = features // fold
    hidden_units = w_gate.shape[1]
    step = fold * LANES
    hidden_steps, down_steps = hidden_units // step, features // step
    down_slots = min(down_steps, 4)
    hidden_bytes, down_bytes = 4 * features * step, 2 * hidden_units * step
    hidden_slots = min(hidden_steps, (WEIGHT_BYTES - down_slots * down_bytes) // hidden_bytes)
    dma = pltpu.SemaphoreType.DMA
    bf16, f32 = jnp.bfloat16, jnp.float32
    half_rows = E * capacity
    weights = 2 * features * hidden_units + hidden_units * features
    return pl.pallas_call(
        functools.partial(fused_kernel, (E, tensor_ranks, capacity, hidden_slots, down_slots)),
        out_shape=jax.ShapeDtypeStruct(resid.shape, bf16),
        in_specs=[pl.BlockSpec(memory_space=pl.ANY)] * 8,
        out_specs=pl.BlockSpec(memory_space=pltpu.VMEM),
        scratch_shapes=[
            pltpu.VMEM(resid.shape, bf16),
            pltpu.VMEM(attn_part.shape, bf16),
            pltpu.VMEM((1, features), f32),
            pltpu.VMEM(w_router.shape, bf16),
            pltpu.VMEM(routes.shape, jnp.int32),
            dma((5,)),
            pltpu.VMEM((hidden_slots, 2, features, step), bf16),
            dma((hidden_slots, 2)),
            pltpu.VMEM((down_slots, hidden_units, step), bf16),
            dma((down_slots,)),
            pltpu.VMEM((tensor_ranks, 2 * rows, features // 2), bf16),
            pltpu.VMEM((tensor_ranks - 1, 2 * rows, features // 2), bf16),
            dma((tensor_ranks - 1,)),
            dma((tensor_ranks - 1,)),
            pltpu.VMEM(resid.shape, f32),
            pltpu.VMEM((fold * rows, E * PACKED_ROWS), f32),
            pltpu.VMEM((E, PACKED_ROWS, width), bf16),
            pltpu.VMEM((2, E, PACKED_ROWS, width), bf16),
            dma((E,)),
            dma((E,)),
            dma((E,)),
            dma((E,)),
            pltpu.VMEM((2 * half_rows, features), bf16),
            pltpu.VMEM((2 * half_rows, hidden_units), bf16),
            pltpu.VMEM((down_steps, 2, half_rows, step), f32),
            pltpu.VMEM((down_steps, half_rows, step), bf16),
            pltpu.VMEM((down_steps, half_rows, step), bf16),
            dma((down_steps,)),
            dma((down_steps,)),
            pltpu.VMEM((down_steps, E, PACKED_ROWS, LANES), bf16),
            pltpu.VMEM((down_steps, E, PACKED_ROWS, LANES), bf16),
            dma((down_steps, E)),
            dma((down_steps, E)),
        ],
        compiler_params=pltpu.CompilerParams(
            collective_id=0, has_side_effects=True, vmem_limit_bytes=VMEM_BYTES
        ),
        cost_estimate=pl.CostEstimate(
            flops=2 * 2 * half_rows * weights,
            bytes_accessed=2 * weights,
            transcendentals=2 * half_rows * hidden_units,
        ),
    )(resid, attn_part, norm_gain.reshape(1, features), w_router, routes, w_gate, w_up, w_down)


def fits(mesh):
    ranks = mesh.shape["expert"] * mesh.shape["tensor"]
    return ranks == 2 * E and mesh.shape["tensor"] % 2 == 0


def solution(mesh):
    return jax.shard_map(
        fused_shards if fits(mesh) else shards,
        mesh=mesh,
        in_specs=(
            P(("groups", "expert", "tensor"), None),
            P(("groups", "expert"), "tensor"),
            P(),
            P(),
            P(("groups", "expert", "tensor"), None),
            P(None, ("expert", "tensor")),
            P(None, ("expert", "tensor")),
            P(("expert", "tensor"), None),
        ),
        out_specs=P(("groups", "expert", "tensor"), None),
        check_vma=False,
    )
```

```python
import functools

import jax
import jax.numpy as jnp
from jax import lax
from jax.experimental import pallas as pl
from jax.experimental.pallas import tpu as pltpu
from jax.sharding import PartitionSpec as P

E = 8
MESH = pl.DeviceIdType.MESH


EPSILON = 1e-05


def partner(shard, axis, distance):
    return lax.ppermute(shard, axis, [(i, i ^ 1 << distance) for i in range(lax.axis_size(axis))])


def shards(resid, attn_part, norm_gain, w_router, routes, w_gate, w_up, w_down):
    expert_ranks = lax.axis_size("expert")
    tensor_ranks = lax.axis_size("tensor")
    my_expert_rank = lax.axis_index("expert")
    my_tensor_rank = lax.axis_index("tensor")
    token_rows = resid.shape[0]
    feature_count = resid.shape[1]
    holders = max(1, expert_ranks // E)
    hosted = max(1, E // expert_ranks)
    expert_groups = E // hosted
    capacity = token_rows // 2
    rank_slots = hosted * capacity
    feature_share = feature_count // holders
    levels = holders.bit_length() - 1
    partial_terms = attn_part.astype(jnp.float32)
    attn_rows = lax.psum_scatter(
        partial_terms.astype(jnp.bfloat16), "tensor", scatter_dimension=0, tiled=True
    ).astype(jnp.float32)
    hidden_state = (resid.astype(jnp.float32) + attn_rows).astype(jnp.bfloat16)
    hidden_wide = lax.optimization_barrier(hidden_state).astype(jnp.float32)
    inverse_rms = lax.rsqrt(jnp.mean(hidden_wide * hidden_wide, axis=1, keepdims=True) + EPSILON)
    normed = (hidden_wide * inverse_rms * norm_gain).astype(jnp.bfloat16)
    logits = jnp.dot(normed, w_router, preferred_element_type=jnp.float32)
    expert_columns = lax.broadcasted_iota(jnp.int32, (token_rows, E), 1)
    pick_first = (routes[:, 0:1] == expert_columns).astype(jnp.float32)
    pick_second = (routes[:, 1:2] == expert_columns).astype(jnp.float32)
    share_first = jax.nn.sigmoid(jnp.sum((pick_first - pick_second) * logits, axis=1))
    share_second = 1.0 - share_first
    row_later = lax.broadcasted_iota(jnp.int32, (token_rows, token_rows), 0)
    row_earlier = lax.broadcasted_iota(jnp.int32, (token_rows, token_rows), 1)
    earlier = (row_later > row_earlier).astype(jnp.float32)
    before = jnp.dot(earlier, pick_first + pick_second, precision=lax.Precision.HIGHEST)
    slot_first = jnp.sum(before * pick_first, axis=1)
    slot_second = jnp.sum(before * pick_second, axis=1)
    slot_numbers = lax.broadcasted_iota(jnp.int32, (token_rows, E, capacity), 2).astype(jnp.float32)
    cell_first = pick_first[:, :, None] * (slot_numbers == slot_first[:, None, None]).astype(
        jnp.float32
    )
    cell_second = pick_second[:, :, None] * (slot_numbers == slot_second[:, None, None]).astype(
        jnp.float32
    )
    placement = (
        (cell_first + cell_second)
        .reshape(token_rows, expert_groups, rank_slots)
        .astype(jnp.bfloat16)
    )
    combine_weight = (
        share_first[:, None, None] * cell_first + share_second[:, None, None] * cell_second
    ).reshape(token_rows, expert_groups, rank_slots)
    outgoing = jnp.einsum(
        "rgc,rd->gcd", placement, normed, preferred_element_type=jnp.float32
    ).astype(jnp.bfloat16)
    outgoing = jnp.repeat(outgoing, holders, axis=0)
    arrived = lax.all_to_all(outgoing, "expert", split_axis=0, concat_axis=0, tiled=True)
    device_span = my_expert_rank * tensor_ranks + my_tensor_rank
    own_expert = device_span * E // (expert_ranks * tensor_ranks)
    local_index = own_expert - my_expert_rank // holders * hosted

    def activate(token_block):
        source_count = token_block.shape[0]
        selected = lax.dynamic_slice_in_dim(token_block, local_index * capacity, capacity, 1)
        flattened = selected.reshape(source_count * capacity, feature_count)
        gate_value = jnp.dot(flattened, w_gate, preferred_element_type=jnp.float32)
        up_value = jnp.dot(flattened, w_up, preferred_element_type=jnp.float32)
        return (jax.nn.silu(gate_value) * up_value).astype(jnp.bfloat16)

    def expert_partial(token_block):
        source_count = token_block.shape[0]
        activated = activate(token_block)
        produced = jnp.dot(activated, w_down, preferred_element_type=jnp.float32).reshape(
            source_count, capacity, feature_count
        )
        if hosted == 1:
            return produced
        blank = jnp.zeros((source_count, rank_slots, feature_count), jnp.float32)
        return lax.dynamic_update_slice_in_dim(blank, produced, local_index * capacity, 1)

    partial_value = expert_partial(lax.all_gather(arrived, "tensor", axis=0, tiled=True))
    leading = partial_value.shape[0]
    layered = partial_value.reshape((leading, rank_slots) + (2,) * levels + (feature_share,))
    remaining = [section for section in range(levels - 1, -1, -1)]
    for section in range(levels):
        split_axis = 2 + remaining.index(section)
        my_side = my_expert_rank // 2**section % 2
        kept_half = lax.dynamic_index_in_dim(layered, my_side, split_axis, keepdims=False)
        given_half = lax.dynamic_index_in_dim(layered, 1 - my_side, split_axis, keepdims=False)
        layered = kept_half + partner(given_half.astype(jnp.bfloat16), "expert", section).astype(
            given_half.dtype
        )
        remaining = [other for other in remaining if other != section]
    own_sources = lax.psum_scatter(
        layered.astype(jnp.bfloat16), "tensor", scatter_dimension=0, tiled=True
    ).astype(jnp.float32)
    returned = lax.all_to_all(
        own_sources.astype(jnp.bfloat16), "expert", split_axis=0, concat_axis=0, tiled=True
    ).astype(own_sources.dtype)
    returned_view = returned.reshape(expert_groups, holders, rank_slots, feature_share)
    mixed = jnp.einsum(
        "rgc,gscp->rsp", combine_weight, returned_view, precision=lax.Precision.HIGHEST
    )
    mixed = mixed.reshape(token_rows, feature_count)
    return (hidden_wide + mixed).astype(jnp.bfloat16)


LANES = 128
PACKED_ROWS = 16
WEIGHT_BYTES = 52 << 20
VMEM_BYTES = 61 << 20


def fused_kernel(
    sizes,
    resid_hbm,
    attn_hbm,
    gain_hbm,
    router_hbm,
    routes_hbm,
    gate_hbm,
    up_hbm,
    down_hbm,
    out_ref,
    resid,
    attn,
    gain,
    router,
    routes,
    in_sem,
    hidden_weights,
    hidden_sem,
    down_weights,
    down_sem,
    attn_out,
    attn_in,
    attn_out_sem,
    attn_in_sem,
    hidden_ref,
    share_ref,
    slots_out,
    slots_in,
    slots_out_sem,
    slots_in_sem,
    pass_out_sem,
    pass_in_sem,
    tokens,
    gate_sum,
    up_sum,
    activated,
    partial_ref,
    half_out,
    half_in,
    half_out_sem,
    half_in_sem,
    back_out,
    back_in,
    back_out_sem,
    back_in_sem,
):
    experts, tensor_ranks, capacity, hidden_slots, down_slots = sizes
    rows, features = resid.shape
    fold = PACKED_ROWS // capacity
    parts = slots_out.shape[0]
    part_features = features // parts
    width = part_features // fold
    hidden_step = hidden_weights.shape[2]
    hidden_steps = features // hidden_step
    part_steps = hidden_steps // parts
    hidden_units = gate_hbm.shape[1]
    down_step = down_weights.shape[2]
    down_steps = features // down_step
    pairs = tensor_ranks // 2
    group = lax.axis_index("groups")
    my_z = lax.axis_index("expert")
    my_t = lax.axis_index("tensor")
    core = my_t % 2
    me = my_z * pairs + my_t // 2
    sibling = (group, my_z, my_t + 1 - 2 * core)

    def holder(number):
        return (group, number // pairs, (number % pairs) * 2 + core)

    def after(step):
        return (me + step) % experts

    def before(step):
        return (me + experts - step) % experts

    small = [
        pltpu.make_async_copy(source, target, in_sem.at[i])
        for i, (source, target) in enumerate(
            (
                (attn_hbm, attn),
                (resid_hbm, resid),
                (gain_hbm, gain),
                (router_hbm, router),
                (routes_hbm, routes),
            )
        )
    ]
    for copy in small:
        copy.start()

    def hidden_copies(step, slot):
        inputs = pl.ds(pl.multiple_of(step * hidden_step, hidden_step), hidden_step)
        return [
            pltpu.make_async_copy(
                source.at[inputs], hidden_weights.at[slot, i], hidden_sem.at[slot, i]
            )
            for i, source in enumerate((gate_hbm, up_hbm))
        ]

    def down_copy(step, slot):
        columns = pl.ds(pl.multiple_of(step * down_step, down_step), down_step)
        return pltpu.make_async_copy(
            down_hbm.at[:, columns], down_weights.at[slot], down_sem.at[slot]
        )

    for step in range(hidden_slots):
        for copy in hidden_copies(step, step):
            copy.start()

    barrier = pltpu.get_barrier_semaphore()
    tensor_peers = [(group, my_z, (my_t + i) % tensor_ranks) for i in range(1, tensor_ranks)]
    peers = [holder(after(i)) for i in range(1, experts)]
    for peer in tensor_peers + peers:
        pl.semaphore_signal(barrier, inc=1, device_id=peer, device_id_type=MESH)

    small[0].wait()
    terms = attn[...].astype(jnp.float32)
    half = features // 2
    for i in range(tensor_ranks):
        block = terms[i * rows : (i + 1) * rows]
        attn_out[i] = jnp.concatenate([block[:, :half], block[:, half:]], axis=0).astype(
            jnp.bfloat16
        )
    pl.semaphore_wait(barrier, len(tensor_peers) + len(peers))

    def attn_copy(step):
        target = (my_t + step) % tensor_ranks
        return pltpu.make_async_remote_copy(
            src_ref=attn_out.at[target],
            dst_ref=attn_in.at[step - 1],
            send_sem=attn_out_sem.at[step - 1],
            recv_sem=attn_in_sem.at[step - 1],
            device_id=(group, my_z, target),
            device_id_type=MESH,
        )

    attn_copies = [attn_copy(step) for step in range(1, tensor_ranks)]
    for copy in attn_copies:
        copy.start()
    for copy in small[1:]:
        copy.wait()
    diagonal = lax.broadcasted_iota(jnp.int32, (rows, rows), 0) == lax.broadcasted_iota(
        jnp.int32, (rows, rows), 1
    )
    first, second = [
        jnp.sum(jnp.where(diagonal, routes[i : i + 1].astype(jnp.float32), 0.0), axis=1, keepdims=True)
        .astype(jnp.int32)
        for i in range(2)
    ]
    columns = lax.broadcasted_iota(jnp.int32, (rows, LANES), 1)
    row_number = lax.broadcasted_iota(jnp.int32, (rows, LANES), 0)
    pick_first = (columns == first).astype(jnp.float32)
    pick_second = (columns == second).astype(jnp.float32)
    both = pick_first + pick_second
    earlier = jnp.zeros((rows, LANES), jnp.float32)
    for i in range(rows):
        earlier += jnp.where(row_number > i, both[i : i + 1], 0.0)
    slot_first = jnp.sum(earlier * pick_first, axis=1, keepdims=True).astype(jnp.int32)
    slot_second = jnp.sum(earlier * pick_second, axis=1, keepdims=True).astype(jnp.int32)
    place_first = jnp.concatenate([first * PACKED_ROWS + slot_first] * fold, axis=0)
    place_second = jnp.concatenate([second * PACKED_ROWS + slot_second] * fold, axis=0)
    packed = experts * PACKED_ROWS
    part = lax.broadcasted_iota(jnp.int32, (fold * rows, packed), 0) // rows * capacity
    cells = lax.broadcasted_iota(jnp.int32, (fold * rows, packed), 1) - part
    cell_first = (cells == place_first).astype(jnp.float32)
    cell_second = (cells == place_second).astype(jnp.float32)
    placement = (cell_first + cell_second).T.astype(jnp.bfloat16)

    summed = attn_out[my_t].astype(jnp.float32)
    for i, copy in enumerate(attn_copies):
        copy.wait_recv()
        summed += attn_in[i].astype(jnp.float32)
    attn_sum = jnp.concatenate([summed[:rows], summed[rows:]], axis=1)
    hidden_wide = (
        (resid[...].astype(jnp.float32) + attn_sum).astype(jnp.bfloat16).astype(jnp.float32)
    )
    hidden_ref[...] = hidden_wide
    mean_square = jnp.sum(hidden_wide * hidden_wide, axis=1, keepdims=True) / features
    normed_wide = hidden_wide * lax.rsqrt(mean_square + EPSILON) * gain[...]
    normed = normed_wide.astype(jnp.bfloat16)

    def slot_copy(part, step):
        return pltpu.make_async_remote_copy(
            src_ref=slots_out.at[part, after(step)],
            dst_ref=slots_in.at[part, core, me],
            send_sem=slots_out_sem.at[part, step],
            recv_sem=slots_in_sem.at[part, step],
            device_id=holder(after(step)),
            device_id_type=MESH,
        )

    def pass_copy(part, step):
        source = slots_out.at[part, me] if step == 0 else slots_in.at[part, core, before(step)]
        return pltpu.make_async_remote_copy(
            src_ref=source,
            dst_ref=slots_in.at[part, core, before(step)],
            send_sem=pass_out_sem.at[part, step],
            recv_sem=pass_in_sem.at[part, step],
            device_id=sibling,
            device_id_type=MESH,
        )

    for part in range(parts):
        start = part * part_features
        folded = jnp.concatenate(
            [
                normed_wide[:, start + i * width : start + (i + 1) * width]
                for i in range(fold)
            ],
            axis=0,
        ).astype(jnp.bfloat16)
        outgoing = jnp.dot(placement, folded, preferred_element_type=jnp.float32)
        slots_out[part] = outgoing.astype(jnp.bfloat16).reshape(experts, PACKED_ROWS, width)
        for step in range(1, experts):
            slot_copy(part, step).start()
        pass_copy(part, 0).start()
        slots_in[part, core, me] = slots_out[part, me]
    for step in range(down_slots):
        down_copy(step, step).start()
    gate_sum[...] = jnp.zeros_like(gate_sum)
    up_sum[...] = jnp.zeros_like(up_sum)

    logits = lax.dot_general(
        normed, router[...], (((1,), (1,)), ((), ())), preferred_element_type=jnp.float32
    )
    expert_columns = lax.broadcasted_iota(jnp.int32, (rows, experts), 1)
    logit_first = jnp.sum(jnp.where(expert_columns == first, logits, 0.0), axis=1, keepdims=True)
    logit_second = jnp.sum(jnp.where(expert_columns == second, logits, 0.0), axis=1, keepdims=True)
    share_first = 1.0 / (1.0 + jnp.exp(logit_second - logit_first))
    share_second = 1.0 - share_first
    share_ref[...] = (
        jnp.concatenate([share_first] * fold, axis=0) * cell_first
        + jnp.concatenate([share_second] * fold, axis=0) * cell_second
    )

    sources = 2 * experts
    token_rows = sources * capacity
    token_number = lax.broadcasted_iota(jnp.int32, (token_rows, sources * PACKED_ROWS), 0)
    packed_number = lax.broadcasted_iota(jnp.int32, (token_rows, sources * PACKED_ROWS), 1)
    wanted = token_number // capacity * PACKED_ROWS + token_number % capacity

    def receive(part):
        for step in range(1, experts):
            slot_copy(part, step).wait_recv()
            pass_copy(part, step).start()
        for step in range(experts):
            pass_copy(part, step).wait_recv()
        arrived = slots_in[part].reshape(sources * PACKED_ROWS, width)
        for i in range(fold):
            select = (packed_number == wanted + i * capacity).astype(jnp.float32)
            place, column = divmod(i * width, hidden_step)
            tokens[part * part_steps + place, :, column : column + width] = jnp.dot(
                select.astype(jnp.bfloat16), arrived, preferred_element_type=jnp.float32
            ).astype(jnp.bfloat16)

    tile = min(hidden_units, 8 * LANES)

    def hidden_body(step, carry):
        slot = step % hidden_slots

        @pl.when(step % part_steps == 0)
        def _():
            receive(step // part_steps)

        for copy in hidden_copies(step, slot):
            copy.wait()
        for i, total in enumerate((gate_sum, up_sum)):
            for start in range(0, hidden_units, tile):
                total[:, start : start + tile] += jnp.dot(
                    tokens[step],
                    hidden_weights[slot, i, :, start : start + tile],
                    preferred_element_type=jnp.float32,
                )

        @pl.when(step + hidden_slots < hidden_steps)
        def _():
            for copy in hidden_copies(step + hidden_slots, slot):
                copy.start()

        return carry

    lax.fori_loop(0, hidden_steps, hidden_body, 0)
    for start in range(0, hidden_units, tile):
        span = slice(start, start + tile)
        gate_value = gate_sum[:, span]
        value = gate_value / (1.0 + jnp.exp(-gate_value)) * up_sum[:, span]
        activated[:, span] = value.astype(jnp.bfloat16)

    half_rows = experts * capacity

    def half_copy(step):
        return pltpu.make_async_remote_copy(
            src_ref=half_out.at[step],
            dst_ref=half_in.at[step],
            send_sem=half_out_sem.at[step],
            recv_sem=half_in_sem.at[step],
            device_id=sibling,
            device_id_type=MESH,
        )

    def back_copy(step, distance):
        return pltpu.make_async_remote_copy(
            src_ref=back_out.at[step, after(distance)],
            dst_ref=back_in.at[step, me],
            send_sem=back_out_sem.at[step, distance],
            recv_sem=back_in_sem.at[step, distance],
            device_id=holder(after(distance)),
            device_id_type=MESH,
        )

    to_row = lax.broadcasted_iota(jnp.int32, (packed, packed), 0)
    from_row = lax.broadcasted_iota(jnp.int32, (packed, packed), 1)
    origin = (
        to_row % PACKED_ROWS // capacity * half_rows
        + to_row // PACKED_ROWS * capacity
        + to_row % capacity
    )
    reorder = (from_row == origin).astype(jnp.float32).astype(jnp.bfloat16)

    def send_back(step):
        half_copy(step).wait_recv()
        total = partial_ref[step, core] + half_in[step].astype(jnp.float32)
        stacked = jnp.concatenate(
            [total[:, i * LANES : (i + 1) * LANES] for i in range(fold)], axis=0
        ).astype(jnp.bfloat16)
        ordered = jnp.dot(reorder, stacked, preferred_element_type=jnp.float32)
        back_out[step] = ordered.astype(jnp.bfloat16).reshape(experts, PACKED_ROWS, LANES)
        for distance in range(1, experts):
            back_copy(step, distance).start()
        back_in[step, me] = back_out[step, me]

    def down_body(step, carry):
        slot = step % down_slots
        down_copy(step, slot).wait()
        produced = jnp.dot(activated[...], down_weights[slot], preferred_element_type=jnp.float32)
        partial_ref[step] = produced.reshape(2, half_rows, down_step)

        @pl.when(step + down_slots < down_steps)
        def _():
            down_copy(step + down_slots, slot).start()

        half_out[step] = partial_ref[step, 1 - core].astype(jnp.bfloat16)
        half_copy(step).start()

        @pl.when(step > 0)
        def _():
            send_back(step - 1)

        return carry

    lax.fori_loop(0, down_steps, down_body, 0)
    send_back(down_steps - 1)

    for step in range(down_steps):
        for distance in range(1, experts):
            back_copy(step, distance).wait_recv()
        mixed = jnp.dot(
            share_ref[...],
            back_in[step].reshape(packed, LANES).astype(jnp.float32),
            precision=lax.Precision.HIGHEST,
            preferred_element_type=jnp.float32,
        )
        for i in range(fold):
            span = slice(step * down_step + i * LANES, step * down_step + (i + 1) * LANES)
            out_ref[:, span] = (
                hidden_ref[:, span] + mixed[i * rows : (i + 1) * rows]
            ).astype(jnp.bfloat16)

    for copy in attn_copies:
        copy.wait_send()
    for part in range(parts):
        for step in range(experts):
            pass_copy(part, step).wait_send()
            if step > 0:
                slot_copy(part, step).wait_send()
    for step in range(down_steps):
        half_copy(step).wait_send()
        for distance in range(1, experts):
            back_copy(step, distance).wait_send()


def fused_shards(resid, attn_part, norm_gain, w_router, routes, w_gate, w_up, w_down):
    tensor_ranks = lax.axis_size("tensor")
    rows, features = resid.shape
    capacity = rows // 2
    fold = PACKED_ROWS // capacity
    hidden_units = w_gate.shape[1]
    step = fold * LANES
    steps = features // step
    parts = steps // 2 if steps % 2 == 0 else steps
    width = features // parts // fold
    hidden_steps, down_steps = steps, steps
    down_slots = min(down_steps, 3)
    hidden_bytes, down_bytes = 4 * hidden_units * step, 2 * hidden_units * step
    hidden_slots = min(hidden_steps, (WEIGHT_BYTES - down_slots * down_bytes) // hidden_bytes)
    dma = pltpu.SemaphoreType.DMA
    bf16, f32 = jnp.bfloat16, jnp.float32
    half_rows = E * capacity
    weights = 2 * features * hidden_units + hidden_units * features
    return pl.pallas_call(
        functools.partial(fused_kernel, (E, tensor_ranks, capacity, hidden_slots, down_slots)),
        out_shape=jax.ShapeDtypeStruct(resid.shape, bf16),
        in_specs=[pl.BlockSpec(memory_space=pl.ANY)] * 8,
        out_specs=pl.BlockSpec(memory_space=pltpu.VMEM),
        scratch_shapes=[
            pltpu.VMEM(resid.shape, bf16),
            pltpu.VMEM(attn_part.shape, bf16),
            pltpu.VMEM((1, features), f32),
            pltpu.VMEM(w_router.shape[::-1], bf16),
            pltpu.VMEM(routes.shape[::-1], jnp.int32),
            dma((5,)),
            pltpu.VMEM((hidden_slots, 2, step, hidden_units), bf16),
            dma((hidden_slots, 2)),
            pltpu.VMEM((down_slots, hidden_units, step), bf16),
            dma((down_slots,)),
            pltpu.VMEM((tensor_ranks, 2 * rows, features // 2), bf16),
            pltpu.VMEM((tensor_ranks - 1, 2 * rows, features // 2), bf16),
            dma((tensor_ranks - 1,)),
            dma((tensor_ranks - 1,)),
            pltpu.VMEM(resid.shape, f32),
            pltpu.VMEM((fold * rows, E * PACKED_ROWS), f32),
            pltpu.VMEM((parts, E, PACKED_ROWS, width), bf16),
            pltpu.VMEM((parts, 2, E, PACKED_ROWS, width), bf16),
            dma((parts, E)),
            dma((parts, E)),
            dma((parts, E)),
            dma((parts, E)),
            pltpu.VMEM((hidden_steps, 2 * half_rows, step), bf16),
            pltpu.VMEM((2 * half_rows, hidden_units), f32),
            pltpu.VMEM((2 * half_rows, hidden_units), f32),
            pltpu.VMEM((2 * half_rows, hidden_units), bf16),
            pltpu.VMEM((down_steps, 2, half_rows, step), f32),
            pltpu.VMEM((down_steps, half_rows, step), bf16),
            pltpu.VMEM((down_steps, half_rows, step), bf16),
            dma((down_steps,)),
            dma((down_steps,)),
            pltpu.VMEM((down_steps, E, PACKED_ROWS, LANES), bf16),
            pltpu.VMEM((down_steps, E, PACKED_ROWS, LANES), bf16),
            dma((down_steps, E)),
            dma((down_steps, E)),
        ],
        compiler_params=pltpu.CompilerParams(
            collective_id=0, has_side_effects=True, vmem_limit_bytes=VMEM_BYTES
        ),
        cost_estimate=pl.CostEstimate(
            flops=2 * 2 * half_rows * weights,
            bytes_accessed=2 * weights,
            transcendentals=2 * half_rows * hidden_units,
        ),
    )(resid, attn_part, norm_gain.reshape(1, features), w_router.T, routes.T, w_gate, w_up, w_down)


def fits(mesh):
    ranks = mesh.shape["expert"] * mesh.shape["tensor"]
    return ranks == 2 * E and mesh.shape["tensor"] % 2 == 0


def solution(mesh):
    return jax.shard_map(
        fused_shards if fits(mesh) else shards,
        mesh=mesh,
        in_specs=(
            P(("groups", "expert", "tensor"), None),
            P(("groups", "expert"), "tensor"),
            P(),
            P(),
            P(("groups", "expert", "tensor"), None),
            P(None, ("expert", "tensor")),
            P(None, ("expert", "tensor")),
            P(("expert", "tensor"), None),
        ),
        out_specs=P(("groups", "expert", "tensor"), None),
        check_vma=False,
    )
```

```python
import functools

import jax
import jax.numpy as jnp
from jax import lax
from jax.experimental import pallas as pl
from jax.experimental.pallas import tpu as pltpu
from jax.sharding import PartitionSpec as P

E = 8
MESH = pl.DeviceIdType.MESH


EPSILON = 1e-05


def partner(shard, axis, distance):
    return lax.ppermute(shard, axis, [(i, i ^ 1 << distance) for i in range(lax.axis_size(axis))])


def shards(resid, attn_part, norm_gain, w_router, routes, w_gate, w_up, w_down):
    expert_ranks = lax.axis_size("expert")
    tensor_ranks = lax.axis_size("tensor")
    my_expert_rank = lax.axis_index("expert")
    my_tensor_rank = lax.axis_index("tensor")
    token_rows = resid.shape[0]
    feature_count = resid.shape[1]
    holders = max(1, expert_ranks // E)
    hosted = max(1, E // expert_ranks)
    expert_groups = E // hosted
    capacity = token_rows // 2
    rank_slots = hosted * capacity
    feature_share = feature_count // holders
    levels = holders.bit_length() - 1
    partial_terms = attn_part.astype(jnp.float32)
    attn_rows = lax.psum_scatter(
        partial_terms.astype(jnp.bfloat16), "tensor", scatter_dimension=0, tiled=True
    ).astype(jnp.float32)
    hidden_state = (resid.astype(jnp.float32) + attn_rows).astype(jnp.bfloat16)
    hidden_wide = lax.optimization_barrier(hidden_state).astype(jnp.float32)
    inverse_rms = lax.rsqrt(jnp.mean(hidden_wide * hidden_wide, axis=1, keepdims=True) + EPSILON)
    normed = (hidden_wide * inverse_rms * norm_gain).astype(jnp.bfloat16)
    logits = jnp.dot(normed, w_router, preferred_element_type=jnp.float32)
    expert_columns = lax.broadcasted_iota(jnp.int32, (token_rows, E), 1)
    pick_first = (routes[:, 0:1] == expert_columns).astype(jnp.float32)
    pick_second = (routes[:, 1:2] == expert_columns).astype(jnp.float32)
    share_first = jax.nn.sigmoid(jnp.sum((pick_first - pick_second) * logits, axis=1))
    share_second = 1.0 - share_first
    row_later = lax.broadcasted_iota(jnp.int32, (token_rows, token_rows), 0)
    row_earlier = lax.broadcasted_iota(jnp.int32, (token_rows, token_rows), 1)
    earlier = (row_later > row_earlier).astype(jnp.float32)
    before = jnp.dot(earlier, pick_first + pick_second, precision=lax.Precision.HIGHEST)
    slot_first = jnp.sum(before * pick_first, axis=1)
    slot_second = jnp.sum(before * pick_second, axis=1)
    slot_numbers = lax.broadcasted_iota(jnp.int32, (token_rows, E, capacity), 2).astype(jnp.float32)
    cell_first = pick_first[:, :, None] * (slot_numbers == slot_first[:, None, None]).astype(
        jnp.float32
    )
    cell_second = pick_second[:, :, None] * (slot_numbers == slot_second[:, None, None]).astype(
        jnp.float32
    )
    placement = (
        (cell_first + cell_second)
        .reshape(token_rows, expert_groups, rank_slots)
        .astype(jnp.bfloat16)
    )
    combine_weight = (
        share_first[:, None, None] * cell_first + share_second[:, None, None] * cell_second
    ).reshape(token_rows, expert_groups, rank_slots)
    outgoing = jnp.einsum(
        "rgc,rd->gcd", placement, normed, preferred_element_type=jnp.float32
    ).astype(jnp.bfloat16)
    outgoing = jnp.repeat(outgoing, holders, axis=0)
    arrived = lax.all_to_all(outgoing, "expert", split_axis=0, concat_axis=0, tiled=True)
    device_span = my_expert_rank * tensor_ranks + my_tensor_rank
    own_expert = device_span * E // (expert_ranks * tensor_ranks)
    local_index = own_expert - my_expert_rank // holders * hosted

    def activate(token_block):
        source_count = token_block.shape[0]
        selected = lax.dynamic_slice_in_dim(token_block, local_index * capacity, capacity, 1)
        flattened = selected.reshape(source_count * capacity, feature_count)
        gate_value = jnp.dot(flattened, w_gate, preferred_element_type=jnp.float32)
        up_value = jnp.dot(flattened, w_up, preferred_element_type=jnp.float32)
        return (jax.nn.silu(gate_value) * up_value).astype(jnp.bfloat16)

    def expert_partial(token_block):
        source_count = token_block.shape[0]
        activated = activate(token_block)
        produced = jnp.dot(activated, w_down, preferred_element_type=jnp.float32).reshape(
            source_count, capacity, feature_count
        )
        if hosted == 1:
            return produced
        blank = jnp.zeros((source_count, rank_slots, feature_count), jnp.float32)
        return lax.dynamic_update_slice_in_dim(blank, produced, local_index * capacity, 1)

    partial_value = expert_partial(lax.all_gather(arrived, "tensor", axis=0, tiled=True))
    leading = partial_value.shape[0]
    layered = partial_value.reshape((leading, rank_slots) + (2,) * levels + (feature_share,))
    remaining = [section for section in range(levels - 1, -1, -1)]
    for section in range(levels):
        split_axis = 2 + remaining.index(section)
        my_side = my_expert_rank // 2**section % 2
        kept_half = lax.dynamic_index_in_dim(layered, my_side, split_axis, keepdims=False)
        given_half = lax.dynamic_index_in_dim(layered, 1 - my_side, split_axis, keepdims=False)
        layered = kept_half + partner(given_half.astype(jnp.bfloat16), "expert", section).astype(
            given_half.dtype
        )
        remaining = [other for other in remaining if other != section]
    own_sources = lax.psum_scatter(
        layered.astype(jnp.bfloat16), "tensor", scatter_dimension=0, tiled=True
    ).astype(jnp.float32)
    returned = lax.all_to_all(
        own_sources.astype(jnp.bfloat16), "expert", split_axis=0, concat_axis=0, tiled=True
    ).astype(own_sources.dtype)
    returned_view = returned.reshape(expert_groups, holders, rank_slots, feature_share)
    mixed = jnp.einsum(
        "rgc,gscp->rsp", combine_weight, returned_view, precision=lax.Precision.HIGHEST
    )
    mixed = mixed.reshape(token_rows, feature_count)
    return (hidden_wide + mixed).astype(jnp.bfloat16)


LANES = 128
PACKED_ROWS = 16
WEIGHT_BYTES = 52 << 20
VMEM_BYTES = 60 << 20


def fused_kernel(
    sizes,
    resid_hbm,
    attn_hbm,
    gain_hbm,
    router_hbm,
    routes_hbm,
    gate_hbm,
    up_hbm,
    down_hbm,
    out_ref,
    resid,
    attn,
    gain,
    router,
    routes,
    in_sem,
    hidden_weights,
    hidden_sem,
    down_weights,
    down_sem,
    attn_out,
    attn_in,
    attn_out_sem,
    attn_in_sem,
    hidden_ref,
    share_ref,
    slots_out,
    slots_in,
    slots_out_sem,
    slots_in_sem,
    pass_out_sem,
    pass_in_sem,
    tokens,
    activated,
    partial_ref,
    half_out,
    half_in,
    half_out_sem,
    half_in_sem,
    back_out,
    back_in,
    back_out_sem,
    back_in_sem,
):
    experts, tensor_ranks, capacity, hidden_slots, down_slots = sizes
    rows, features = resid.shape
    fold = PACKED_ROWS // capacity
    width = features // fold
    hidden_step = hidden_weights.shape[3]
    hidden_steps = gate_hbm.shape[1] // hidden_step
    down_step = down_weights.shape[2]
    chunks, _, _, chunk = partial_ref.shape
    chunk_steps = chunk // down_step
    down_steps = chunks * chunk_steps
    span = chunk // fold
    pairs = tensor_ranks // 2
    group = lax.axis_index("groups")
    my_z = lax.axis_index("expert")
    my_t = lax.axis_index("tensor")
    core = my_t % 2
    me = my_z * pairs + my_t // 2
    sibling = (group, my_z, my_t + 1 - 2 * core)

    def holder(number):
        return (group, number // pairs, (number % pairs) * 2 + core)

    def after(step):
        return (me + step) % experts

    def before(step):
        return (me + experts - step) % experts

    small = [
        pltpu.make_async_copy(source, target, in_sem.at[i])
        for i, (source, target) in enumerate(
            (
                (attn_hbm, attn),
                (resid_hbm, resid),
                (gain_hbm, gain),
                (router_hbm, router),
                (routes_hbm, routes),
            )
        )
    ]
    for copy in small:
        copy.start()

    barrier = pltpu.get_barrier_semaphore()
    tensor_peers = [(group, my_z, (my_t + i) % tensor_ranks) for i in range(1, tensor_ranks, 2)]
    peers = [holder(after(i)) for i in range(1, experts)]
    for peer in tensor_peers + peers:
        pl.semaphore_signal(barrier, inc=1, device_id=peer, device_id_type=MESH)

    def hidden_copies(step, slot):
        columns = pl.ds(pl.multiple_of(step * hidden_step, hidden_step), hidden_step)
        return [
            pltpu.make_async_copy(
                source.at[:, columns], hidden_weights.at[slot, i], hidden_sem.at[slot, i]
            )
            for i, source in enumerate((gate_hbm, up_hbm))
        ]

    def down_copy(step, slot):
        columns = pl.ds(pl.multiple_of(step * down_step, down_step), down_step)
        return pltpu.make_async_copy(
            down_hbm.at[:, columns], down_weights.at[slot], down_sem.at[slot]
        )

    for step in range(hidden_slots):
        for copy in hidden_copies(step, step):
            copy.start()

    small[0].wait()
    terms = attn[...].astype(jnp.float32)
    half = features // 2
    for i in range(tensor_ranks):
        block = terms[i * rows : (i + 1) * rows]
        attn_out[i] = jnp.concatenate([block[:, :half], block[:, half:]], axis=0).astype(
            jnp.bfloat16
        )
    pl.semaphore_wait(barrier, len(tensor_peers) + len(peers))

    def attn_copy(step):
        target = (my_t + step) % tensor_ranks
        return pltpu.make_async_remote_copy(
            src_ref=attn_out.at[target],
            dst_ref=attn_in.at[step - 1],
            send_sem=attn_out_sem.at[step - 1],
            recv_sem=attn_in_sem.at[step - 1],
            device_id=(group, my_z, target),
            device_id_type=MESH,
        )

    attn_copies = [attn_copy(step) for step in range(1, tensor_ranks)]
    for copy in attn_copies:
        copy.start()
    for copy in small[1:]:
        copy.wait()
    diagonal = lax.broadcasted_iota(jnp.int32, (rows, rows), 0) == lax.broadcasted_iota(
        jnp.int32, (rows, rows), 1
    )
    first, second = [
        jnp.sum(jnp.where(diagonal, routes[i : i + 1].astype(jnp.float32), 0.0), axis=1, keepdims=True)
        .astype(jnp.int32)
        for i in range(2)
    ]
    columns = lax.broadcasted_iota(jnp.int32, (rows, LANES), 1)
    row_number = lax.broadcasted_iota(jnp.int32, (rows, LANES), 0)
    pick_first = (columns == first).astype(jnp.float32)
    pick_second = (columns == second).astype(jnp.float32)
    both = pick_first + pick_second
    earlier = jnp.zeros((rows, LANES), jnp.float32)
    for i in range(rows):
        earlier += jnp.where(row_number > i, both[i : i + 1], 0.0)
    slot_first = jnp.sum(earlier * pick_first, axis=1, keepdims=True).astype(jnp.int32)
    slot_second = jnp.sum(earlier * pick_second, axis=1, keepdims=True).astype(jnp.int32)
    place_first = jnp.concatenate([first * PACKED_ROWS + slot_first] * fold, axis=0)
    place_second = jnp.concatenate([second * PACKED_ROWS + slot_second] * fold, axis=0)
    packed = experts * PACKED_ROWS
    part = lax.broadcasted_iota(jnp.int32, (fold * rows, packed), 0) // rows * capacity
    cells = lax.broadcasted_iota(jnp.int32, (fold * rows, packed), 1) - part
    cell_first = (cells == place_first).astype(jnp.float32)
    cell_second = (cells == place_second).astype(jnp.float32)
    placement = (cell_first + cell_second).T.astype(jnp.bfloat16)

    summed = attn_out[my_t].astype(jnp.float32)
    for i, copy in enumerate(attn_copies):
        copy.wait_recv()
        summed += attn_in[i].astype(jnp.float32)
    attn_sum = jnp.concatenate([summed[:rows], summed[rows:]], axis=1)
    hidden_wide = (
        (resid[...].astype(jnp.float32) + attn_sum).astype(jnp.bfloat16).astype(jnp.float32)
    )
    hidden_ref[...] = hidden_wide
    mean_square = jnp.sum(hidden_wide * hidden_wide, axis=1, keepdims=True) / features
    normed_wide = hidden_wide * lax.rsqrt(mean_square + EPSILON) * gain[...]
    normed = normed_wide.astype(jnp.bfloat16)
    folded = jnp.concatenate(
        [normed_wide[:, i * width : (i + 1) * width] for i in range(fold)], axis=0
    ).astype(jnp.bfloat16)
    outgoing = jnp.dot(placement, folded, preferred_element_type=jnp.float32)
    slots_out[...] = outgoing.astype(jnp.bfloat16).reshape(experts, PACKED_ROWS, width)

    def slot_copy(step):
        return pltpu.make_async_remote_copy(
            src_ref=slots_out.at[after(step)],
            dst_ref=slots_in.at[core, me],
            send_sem=slots_out_sem,
            recv_sem=slots_in_sem,
            device_id=holder(after(step)),
            device_id_type=MESH,
        )

    others = pl.ds(0, experts - 1)
    all_slots = pltpu.make_async_remote_copy(
        src_ref=slots_out.at[others],
        dst_ref=slots_in.at[core, others],
        send_sem=slots_out_sem,
        recv_sem=slots_in_sem,
        device_id=sibling,
        device_id_type=MESH,
    )
    pass_copy = pltpu.make_async_remote_copy(
        src_ref=slots_in.at[core],
        dst_ref=slots_in.at[core],
        send_sem=pass_out_sem,
        recv_sem=pass_in_sem,
        device_id=sibling,
        device_id_type=MESH,
    )
    for step in range(1, experts):
        slot_copy(step).start()
    for step in range(down_slots):
        down_copy(step, step).start()
    slots_in[core, me] = slots_out[me]

    logits = lax.dot_general(
        normed, router[...], (((1,), (1,)), ((), ())), preferred_element_type=jnp.float32
    )
    expert_columns = lax.broadcasted_iota(jnp.int32, (rows, experts), 1)
    logit_first = jnp.sum(jnp.where(expert_columns == first, logits, 0.0), axis=1, keepdims=True)
    logit_second = jnp.sum(jnp.where(expert_columns == second, logits, 0.0), axis=1, keepdims=True)
    share_first = 1.0 / (1.0 + jnp.exp(logit_second - logit_first))
    share_second = 1.0 - share_first
    share_ref[...] = (
        jnp.concatenate([share_first] * fold, axis=0) * cell_first
        + jnp.concatenate([share_second] * fold, axis=0) * cell_second
    )

    all_slots.wait_recv()
    pass_copy.start()
    pass_copy.wait_recv()

    sources = 2 * experts
    token_rows = sources * capacity
    arrived = slots_in[...].reshape(sources * PACKED_ROWS, width)
    token_number = lax.broadcasted_iota(jnp.int32, (token_rows, sources * PACKED_ROWS), 0)
    packed_number = lax.broadcasted_iota(jnp.int32, (token_rows, sources * PACKED_ROWS), 1)
    wanted = token_number // capacity * PACKED_ROWS + token_number % capacity
    for i in range(fold):
        select = (packed_number == wanted + i * capacity).astype(jnp.float32).astype(jnp.bfloat16)
        tokens[:, i * width : (i + 1) * width] = jnp.dot(
            select, arrived, preferred_element_type=jnp.float32
        ).astype(jnp.bfloat16)

    def hidden_body(step, carry):
        slot = step % hidden_slots
        for copy in hidden_copies(step, slot):
            copy.wait()
        gate_value = jnp.dot(
            tokens[...], hidden_weights[slot, 0], preferred_element_type=jnp.float32
        )
        up_value = jnp.dot(tokens[...], hidden_weights[slot, 1], preferred_element_type=jnp.float32)
        value = gate_value / (1.0 + jnp.exp(-gate_value)) * up_value
        activated[:, pl.ds(pl.multiple_of(step * hidden_step, hidden_step), hidden_step)] = (
            value.astype(jnp.bfloat16)
        )

        @pl.when(step + hidden_slots < hidden_steps)
        def _():
            for copy in hidden_copies(step + hidden_slots, slot):
                copy.start()

        return carry

    lax.fori_loop(0, hidden_steps, hidden_body, 0)

    half_rows = experts * capacity

    def half_copy(step):
        return pltpu.make_async_remote_copy(
            src_ref=half_out.at[step],
            dst_ref=half_in.at[step],
            send_sem=half_out_sem.at[step],
            recv_sem=half_in_sem.at[step],
            device_id=sibling,
            device_id_type=MESH,
        )

    def back_copy(step, distance):
        return pltpu.make_async_remote_copy(
            src_ref=back_out.at[step, after(distance)],
            dst_ref=back_in.at[step, me],
            send_sem=back_out_sem.at[step],
            recv_sem=back_in_sem.at[step],
            device_id=holder(after(distance)),
            device_id_type=MESH,
        )

    def all_back(step):
        return pltpu.make_async_remote_copy(
            src_ref=back_out.at[step, others],
            dst_ref=back_in.at[step, others],
            send_sem=back_out_sem.at[step],
            recv_sem=back_in_sem.at[step],
            device_id=sibling,
            device_id_type=MESH,
        )

    to_row = lax.broadcasted_iota(jnp.int32, (packed, packed), 0)
    from_row = lax.broadcasted_iota(jnp.int32, (packed, packed), 1)
    origin = (
        to_row % PACKED_ROWS // capacity * half_rows
        + to_row // PACKED_ROWS * capacity
        + to_row % capacity
    )
    reorder = (from_row == origin).astype(jnp.float32).astype(jnp.bfloat16)

    def send_back(step):
        half_copy(step).wait_recv()
        total = partial_ref[step, core] + half_in[step].astype(jnp.float32)
        stacked = jnp.concatenate(
            [total[:, i * span : (i + 1) * span] for i in range(fold)], axis=0
        ).astype(jnp.bfloat16)
        ordered = jnp.dot(reorder, stacked, preferred_element_type=jnp.float32)
        back_out[step] = ordered.astype(jnp.bfloat16).reshape(experts, PACKED_ROWS, span)
        for distance in range(1, experts):
            back_copy(step, distance).start()
        back_in[step, me] = back_out[step, me]

    def down_body(step, carry):
        for i in range(chunk_steps):
            piece = step * chunk_steps + i
            slot = piece % down_slots
            down_copy(piece, slot).wait()
            produced = jnp.dot(
                activated[...], down_weights[slot], preferred_element_type=jnp.float32
            )
            partial_ref[step, :, :, i * down_step : (i + 1) * down_step] = produced.reshape(
                2, half_rows, down_step
            )

            @pl.when(piece + down_slots < down_steps)
            def _():
                down_copy(piece + down_slots, slot).start()

            if i == 0:

                @pl.when(step > 0)
                def _():
                    send_back(step - 1)

        half_out[step] = partial_ref[step, 1 - core].astype(jnp.bfloat16)
        half_copy(step).start()
        return carry

    lax.fori_loop(0, chunks, down_body, 0)
    send_back(chunks - 1)

    for step in range(chunks):
        all_back(step).wait_recv()
        mixed = jnp.dot(
            share_ref[...],
            back_in[step].reshape(packed, span).astype(jnp.float32),
            precision=lax.Precision.HIGHEST,
            preferred_element_type=jnp.float32,
        )
        for i in range(fold):
            where = slice(step * chunk + i * span, step * chunk + (i + 1) * span)
            out_ref[:, where] = (
                hidden_ref[:, where] + mixed[i * rows : (i + 1) * rows]
            ).astype(jnp.bfloat16)

    for copy in attn_copies + [all_slots, pass_copy]:
        copy.wait_send()
    for step in range(chunks):
        half_copy(step).wait_send()
        all_back(step).wait_send()


def fused_shards(resid, attn_part, norm_gain, w_router, routes, w_gate, w_up, w_down):
    tensor_ranks = lax.axis_size("tensor")
    rows, features = resid.shape
    capacity = rows // 2
    fold = PACKED_ROWS // capacity
    width = features // fold
    hidden_units = w_gate.shape[1]
    step = fold * LANES
    hidden_steps, down_steps = hidden_units // step, features // step
    down_slots = min(down_steps, 4)
    chunk = 2 * step if down_steps % 2 == 0 else step
    chunks = features // chunk
    hidden_bytes, down_bytes = 4 * features * step, 2 * hidden_units * step
    hidden_slots = min(hidden_steps, (WEIGHT_BYTES - down_slots * down_bytes) // hidden_bytes)
    dma = pltpu.SemaphoreType.DMA
    bf16, f32 = jnp.bfloat16, jnp.float32
    half_rows = E * capacity
    weights = 2 * features * hidden_units + hidden_units * features
    return pl.pallas_call(
        functools.partial(fused_kernel, (E, tensor_ranks, capacity, hidden_slots, down_slots)),
        out_shape=jax.ShapeDtypeStruct(resid.shape, bf16),
        in_specs=[pl.BlockSpec(memory_space=pl.ANY)] * 8,
        out_specs=pl.BlockSpec(memory_space=pltpu.VMEM),
        scratch_shapes=[
            pltpu.VMEM(resid.shape, bf16),
            pltpu.VMEM(attn_part.shape, bf16),
            pltpu.VMEM((1, features), f32),
            pltpu.VMEM(w_router.shape[::-1], bf16),
            pltpu.VMEM(routes.shape[::-1], jnp.int32),
            dma((5,)),
            pltpu.VMEM((hidden_slots, 2, features, step), bf16),
            dma((hidden_slots, 2)),
            pltpu.VMEM((down_slots, hidden_units, step), bf16),
            dma((down_slots,)),
            pltpu.VMEM((tensor_ranks, 2 * rows, features // 2), bf16),
            pltpu.VMEM((tensor_ranks - 1, 2 * rows, features // 2), bf16),
            dma((tensor_ranks - 1,)),
            dma((tensor_ranks - 1,)),
            pltpu.VMEM(resid.shape, f32),
            pltpu.VMEM((fold * rows, E * PACKED_ROWS), f32),
            pltpu.VMEM((E, PACKED_ROWS, width), bf16),
            pltpu.VMEM((2, E, PACKED_ROWS, width), bf16),
            dma(()),
            dma(()),
            dma(()),
            dma(()),
            pltpu.VMEM((2 * half_rows, features), bf16),
            pltpu.VMEM((2 * half_rows, hidden_units), bf16),
            pltpu.VMEM((chunks, 2, half_rows, chunk), f32),
            pltpu.VMEM((chunks, half_rows, chunk), bf16),
            pltpu.VMEM((chunks, half_rows, chunk), bf16),
            dma((chunks,)),
            dma((chunks,)),
            pltpu.VMEM((chunks, E, PACKED_ROWS, chunk // fold), bf16),
            pltpu.VMEM((chunks, E, PACKED_ROWS, chunk // fold), bf16),
            dma((chunks,)),
            dma((chunks,)),
        ],
        compiler_params=pltpu.CompilerParams(
            collective_id=0, has_side_effects=True, vmem_limit_bytes=VMEM_BYTES
        ),
        cost_estimate=pl.CostEstimate(
            flops=2 * 2 * half_rows * weights,
            bytes_accessed=2 * weights,
            transcendentals=2 * half_rows * hidden_units,
        ),
    )(resid, attn_part, norm_gain.reshape(1, features), w_router.T, routes.T, w_gate, w_up, w_down)


def fits(mesh):
    ranks = mesh.shape["expert"] * mesh.shape["tensor"]
    return ranks == 2 * E and mesh.shape["tensor"] % 2 == 0


def solution(mesh):
    return jax.shard_map(
        fused_shards if fits(mesh) else shards,
        mesh=mesh,
        in_specs=(
            P(("groups", "expert", "tensor"), None),
            P(("groups", "expert"), "tensor"),
            P(),
            P(),
            P(("groups", "expert", "tensor"), None),
            P(None, ("expert", "tensor")),
            P(None, ("expert", "tensor")),
            P(("expert", "tensor"), None),
        ),
        out_specs=P(("groups", "expert", "tensor"), None),
        check_vma=False,
    )
```

```python
import functools

import jax
import jax.numpy as jnp
from jax import lax
from jax.experimental import pallas as pl
from jax.experimental.pallas import tpu as pltpu
from jax.sharding import PartitionSpec as P

E = 8
MESH = pl.DeviceIdType.MESH


EPSILON = 1e-05


def partner(shard, axis, distance):
    return lax.ppermute(shard, axis, [(i, i ^ 1 << distance) for i in range(lax.axis_size(axis))])


def shards(resid, attn_part, norm_gain, w_router, routes, w_gate, w_up, w_down):
    expert_ranks = lax.axis_size("expert")
    tensor_ranks = lax.axis_size("tensor")
    my_expert_rank = lax.axis_index("expert")
    my_tensor_rank = lax.axis_index("tensor")
    token_rows = resid.shape[0]
    feature_count = resid.shape[1]
    holders = max(1, expert_ranks // E)
    hosted = max(1, E // expert_ranks)
    expert_groups = E // hosted
    capacity = token_rows // 2
    rank_slots = hosted * capacity
    feature_share = feature_count // holders
    levels = holders.bit_length() - 1
    partial_terms = attn_part.astype(jnp.float32)
    attn_rows = lax.psum_scatter(
        partial_terms.astype(jnp.bfloat16), "tensor", scatter_dimension=0, tiled=True
    ).astype(jnp.float32)
    hidden_state = (resid.astype(jnp.float32) + attn_rows).astype(jnp.bfloat16)
    hidden_wide = lax.optimization_barrier(hidden_state).astype(jnp.float32)
    inverse_rms = lax.rsqrt(jnp.mean(hidden_wide * hidden_wide, axis=1, keepdims=True) + EPSILON)
    normed = (hidden_wide * inverse_rms * norm_gain).astype(jnp.bfloat16)
    logits = jnp.dot(normed, w_router, preferred_element_type=jnp.float32)
    expert_columns = lax.broadcasted_iota(jnp.int32, (token_rows, E), 1)
    pick_first = (routes[:, 0:1] == expert_columns).astype(jnp.float32)
    pick_second = (routes[:, 1:2] == expert_columns).astype(jnp.float32)
    share_first = jax.nn.sigmoid(jnp.sum((pick_first - pick_second) * logits, axis=1))
    share_second = 1.0 - share_first
    row_later = lax.broadcasted_iota(jnp.int32, (token_rows, token_rows), 0)
    row_earlier = lax.broadcasted_iota(jnp.int32, (token_rows, token_rows), 1)
    earlier = (row_later > row_earlier).astype(jnp.float32)
    before = jnp.dot(earlier, pick_first + pick_second, precision=lax.Precision.HIGHEST)
    slot_first = jnp.sum(before * pick_first, axis=1)
    slot_second = jnp.sum(before * pick_second, axis=1)
    slot_numbers = lax.broadcasted_iota(jnp.int32, (token_rows, E, capacity), 2).astype(jnp.float32)
    cell_first = pick_first[:, :, None] * (slot_numbers == slot_first[:, None, None]).astype(
        jnp.float32
    )
    cell_second = pick_second[:, :, None] * (slot_numbers == slot_second[:, None, None]).astype(
        jnp.float32
    )
    placement = (
        (cell_first + cell_second)
        .reshape(token_rows, expert_groups, rank_slots)
        .astype(jnp.bfloat16)
    )
    combine_weight = (
        share_first[:, None, None] * cell_first + share_second[:, None, None] * cell_second
    ).reshape(token_rows, expert_groups, rank_slots)
    outgoing = jnp.einsum(
        "rgc,rd->gcd", placement, normed, preferred_element_type=jnp.float32
    ).astype(jnp.bfloat16)
    outgoing = jnp.repeat(outgoing, holders, axis=0)
    arrived = lax.all_to_all(outgoing, "expert", split_axis=0, concat_axis=0, tiled=True)
    device_span = my_expert_rank * tensor_ranks + my_tensor_rank
    own_expert = device_span * E // (expert_ranks * tensor_ranks)
    local_index = own_expert - my_expert_rank // holders * hosted

    def activate(token_block):
        source_count = token_block.shape[0]
        selected = lax.dynamic_slice_in_dim(token_block, local_index * capacity, capacity, 1)
        flattened = selected.reshape(source_count * capacity, feature_count)
        gate_value = jnp.dot(flattened, w_gate, preferred_element_type=jnp.float32)
        up_value = jnp.dot(flattened, w_up, preferred_element_type=jnp.float32)
        return (jax.nn.silu(gate_value) * up_value).astype(jnp.bfloat16)

    def expert_partial(token_block):
        source_count = token_block.shape[0]
        activated = activate(token_block)
        produced = jnp.dot(activated, w_down, preferred_element_type=jnp.float32).reshape(
            source_count, capacity, feature_count
        )
        if hosted == 1:
            return produced
        blank = jnp.zeros((source_count, rank_slots, feature_count), jnp.float32)
        return lax.dynamic_update_slice_in_dim(blank, produced, local_index * capacity, 1)

    partial_value = expert_partial(lax.all_gather(arrived, "tensor", axis=0, tiled=True))
    leading = partial_value.shape[0]
    layered = partial_value.reshape((leading, rank_slots) + (2,) * levels + (feature_share,))
    remaining = [section for section in range(levels - 1, -1, -1)]
    for section in range(levels):
        split_axis = 2 + remaining.index(section)
        my_side = my_expert_rank // 2**section % 2
        kept_half = lax.dynamic_index_in_dim(layered, my_side, split_axis, keepdims=False)
        given_half = lax.dynamic_index_in_dim(layered, 1 - my_side, split_axis, keepdims=False)
        layered = kept_half + partner(given_half.astype(jnp.bfloat16), "expert", section).astype(
            given_half.dtype
        )
        remaining = [other for other in remaining if other != section]
    own_sources = lax.psum_scatter(
        layered.astype(jnp.bfloat16), "tensor", scatter_dimension=0, tiled=True
    ).astype(jnp.float32)
    returned = lax.all_to_all(
        own_sources.astype(jnp.bfloat16), "expert", split_axis=0, concat_axis=0, tiled=True
    ).astype(own_sources.dtype)
    returned_view = returned.reshape(expert_groups, holders, rank_slots, feature_share)
    mixed = jnp.einsum(
        "rgc,gscp->rsp", combine_weight, returned_view, precision=lax.Precision.HIGHEST
    )
    mixed = mixed.reshape(token_rows, feature_count)
    return (hidden_wide + mixed).astype(jnp.bfloat16)


LANES = 128
PACKED_ROWS = 16
WEIGHT_BYTES = 52 << 20
VMEM_BYTES = 60 << 20


def fused_kernel(
    sizes,
    resid_hbm,
    attn_hbm,
    gain_hbm,
    router_hbm,
    routes_hbm,
    gate_hbm,
    up_hbm,
    down_hbm,
    out_ref,
    resid,
    attn,
    gain,
    router,
    routes,
    in_sem,
    hidden_weights,
    hidden_sem,
    down_weights,
    down_sem,
    attn_out,
    attn_in,
    attn_out_sem,
    attn_in_sem,
    hidden_ref,
    share_ref,
    slots_out,
    slots_in,
    slots_out_sem,
    slots_in_sem,
    pass_out_sem,
    pass_in_sem,
    select,
    reorder,
    tokens,
    activated,
    partial_ref,
    half_out,
    half_in,
    half_out_sem,
    half_in_sem,
    back_out,
    back_in,
    back_out_sem,
    back_in_sem,
):
    experts, tensor_ranks, capacity, hidden_slots, down_slots = sizes
    rows, features = resid.shape
    fold = PACKED_ROWS // capacity
    width = features // fold
    hidden_step = hidden_weights.shape[3]
    hidden_steps = gate_hbm.shape[1] // hidden_step
    down_step = down_weights.shape[2]
    chunks, _, _, chunk = partial_ref.shape
    chunk_steps = chunk // down_step
    down_steps = chunks * chunk_steps
    span = chunk // fold
    pairs = tensor_ranks // 2
    group = lax.axis_index("groups")
    my_z = lax.axis_index("expert")
    my_t = lax.axis_index("tensor")
    core = my_t % 2
    me = my_z * pairs + my_t // 2
    sibling = (group, my_z, my_t + 1 - 2 * core)

    def holder(number):
        return (group, number // pairs, (number % pairs) * 2 + core)

    def after(step):
        return (me + step) % experts

    def before(step):
        return (me + experts - step) % experts

    small = [
        pltpu.make_async_copy(source, target, in_sem.at[i])
        for i, (source, target) in enumerate(
            (
                (attn_hbm, attn),
                (resid_hbm, resid),
                (gain_hbm, gain),
                (router_hbm, router),
                (routes_hbm, routes),
            )
        )
    ]
    for copy in small:
        copy.start()

    barrier = pltpu.get_barrier_semaphore()
    tensor_peers = [(group, my_z, (my_t + i) % tensor_ranks) for i in range(1, tensor_ranks, 2)]
    peers = [holder(after(i)) for i in range(1, experts)]
    for peer in tensor_peers + peers:
        pl.semaphore_signal(barrier, inc=1, device_id=peer, device_id_type=MESH)

    def hidden_copies(step, slot):
        columns = pl.ds(pl.multiple_of(step * hidden_step, hidden_step), hidden_step)
        return [
            pltpu.make_async_copy(
                source.at[:, columns], hidden_weights.at[slot, i], hidden_sem.at[slot, i]
            )
            for i, source in enumerate((gate_hbm, up_hbm))
        ]

    def down_copy(step, slot):
        columns = pl.ds(pl.multiple_of(step * down_step, down_step), down_step)
        return pltpu.make_async_copy(
            down_hbm.at[:, columns], down_weights.at[slot], down_sem.at[slot]
        )

    def start_hidden(step):
        for copy in hidden_copies(step, step):
            copy.start()

    start_hidden(0)
    small[0].wait()
    terms = attn[...].astype(jnp.float32)
    half = features // 2
    for i in range(tensor_ranks):
        block = terms[i * rows : (i + 1) * rows]
        attn_out[i] = jnp.concatenate([block[:, :half], block[:, half:]], axis=0).astype(
            jnp.bfloat16
        )
    pl.semaphore_wait(barrier, len(tensor_peers) + len(peers))

    def attn_copy(step):
        target = (my_t + step) % tensor_ranks
        return pltpu.make_async_remote_copy(
            src_ref=attn_out.at[target],
            dst_ref=attn_in.at[step - 1],
            send_sem=attn_out_sem.at[step - 1],
            recv_sem=attn_in_sem.at[step - 1],
            device_id=(group, my_z, target),
            device_id_type=MESH,
        )

    attn_copies = [attn_copy(step) for step in range(1, tensor_ranks)]
    for copy in attn_copies:
        copy.start()
    for step in range(1, min(2, hidden_slots)):
        start_hidden(step)
    for copy in small[1:]:
        copy.wait()
    diagonal = lax.broadcasted_iota(jnp.int32, (rows, rows), 0) == lax.broadcasted_iota(
        jnp.int32, (rows, rows), 1
    )
    first, second = [
        jnp.sum(jnp.where(diagonal, routes[i : i + 1].astype(jnp.float32), 0.0), axis=1, keepdims=True)
        .astype(jnp.int32)
        for i in range(2)
    ]
    columns = lax.broadcasted_iota(jnp.int32, (rows, LANES), 1)
    row_number = lax.broadcasted_iota(jnp.int32, (rows, LANES), 0)
    pick_first = (columns == first).astype(jnp.float32)
    pick_second = (columns == second).astype(jnp.float32)
    both = pick_first + pick_second
    earlier = jnp.zeros((rows, LANES), jnp.float32)
    for i in range(rows):
        earlier += jnp.where(row_number > i, both[i : i + 1], 0.0)
    slot_first = jnp.sum(earlier * pick_first, axis=1, keepdims=True).astype(jnp.int32)
    slot_second = jnp.sum(earlier * pick_second, axis=1, keepdims=True).astype(jnp.int32)
    place_first = jnp.concatenate([first * PACKED_ROWS + slot_first] * fold, axis=0)
    place_second = jnp.concatenate([second * PACKED_ROWS + slot_second] * fold, axis=0)
    packed = experts * PACKED_ROWS
    part = lax.broadcasted_iota(jnp.int32, (fold * rows, packed), 0) // rows * capacity
    cells = lax.broadcasted_iota(jnp.int32, (fold * rows, packed), 1) - part
    cell_first = (cells == place_first).astype(jnp.float32)
    cell_second = (cells == place_second).astype(jnp.float32)
    placement = (cell_first + cell_second).T.astype(jnp.bfloat16)

    summed = attn_out[my_t].astype(jnp.float32)
    for i, copy in enumerate(attn_copies):
        copy.wait_recv()
        summed += attn_in[i].astype(jnp.float32)
    attn_sum = jnp.concatenate([summed[:rows], summed[rows:]], axis=1)
    hidden_wide = (
        (resid[...].astype(jnp.float32) + attn_sum).astype(jnp.bfloat16).astype(jnp.float32)
    )
    hidden_ref[...] = hidden_wide
    mean_square = jnp.sum(hidden_wide * hidden_wide, axis=1, keepdims=True) / features
    normed_wide = hidden_wide * lax.rsqrt(mean_square + EPSILON) * gain[...]
    normed = normed_wide.astype(jnp.bfloat16)
    folded = jnp.concatenate(
        [normed_wide[:, i * width : (i + 1) * width] for i in range(fold)], axis=0
    ).astype(jnp.bfloat16)
    outgoing = jnp.dot(placement, folded, preferred_element_type=jnp.float32)
    slots_out[...] = outgoing.astype(jnp.bfloat16).reshape(experts, PACKED_ROWS, width)

    def slot_copy(step):
        return pltpu.make_async_remote_copy(
            src_ref=slots_out.at[after(step)],
            dst_ref=slots_in.at[core, me],
            send_sem=slots_out_sem,
            recv_sem=slots_in_sem,
            device_id=holder(after(step)),
            device_id_type=MESH,
        )

    others = pl.ds(0, experts - 1)
    all_slots = pltpu.make_async_remote_copy(
        src_ref=slots_out.at[others],
        dst_ref=slots_in.at[core, others],
        send_sem=slots_out_sem,
        recv_sem=slots_in_sem,
        device_id=sibling,
        device_id_type=MESH,
    )
    pass_copy = pltpu.make_async_remote_copy(
        src_ref=slots_in.at[core],
        dst_ref=slots_in.at[core],
        send_sem=pass_out_sem,
        recv_sem=pass_in_sem,
        device_id=sibling,
        device_id_type=MESH,
    )
    for step in sorted(range(1, experts), key=lambda step: abs(2 * step - experts - 1)):
        slot_copy(step).start()
    for step in range(2, hidden_slots):
        start_hidden(step)
    for step in range(down_slots):
        down_copy(step, step).start()
    slots_in[core, me] = slots_out[me]

    logits = lax.dot_general(
        normed, router[...], (((1,), (1,)), ((), ())), preferred_element_type=jnp.float32
    )
    expert_columns = lax.broadcasted_iota(jnp.int32, (rows, experts), 1)
    logit_first = jnp.sum(jnp.where(expert_columns == first, logits, 0.0), axis=1, keepdims=True)
    logit_second = jnp.sum(jnp.where(expert_columns == second, logits, 0.0), axis=1, keepdims=True)
    share_first = 1.0 / (1.0 + jnp.exp(logit_second - logit_first))
    share_second = 1.0 - share_first
    share_ref[...] = (
        jnp.concatenate([share_first] * fold, axis=0) * cell_first
        + jnp.concatenate([share_second] * fold, axis=0) * cell_second
    )

    sources = 2 * experts
    token_rows = sources * capacity
    token_number = lax.broadcasted_iota(jnp.int32, (token_rows, sources * PACKED_ROWS), 0)
    packed_number = lax.broadcasted_iota(jnp.int32, (token_rows, sources * PACKED_ROWS), 1)
    wanted = token_number // capacity * PACKED_ROWS + token_number % capacity
    for i in range(fold):
        select[i] = (
            (packed_number == wanted + i * capacity).astype(jnp.float32).astype(jnp.bfloat16)
        )
    half_rows = experts * capacity
    to_row = lax.broadcasted_iota(jnp.int32, (packed, packed), 0)
    from_row = lax.broadcasted_iota(jnp.int32, (packed, packed), 1)
    origin = (
        to_row % PACKED_ROWS // capacity * half_rows
        + to_row // PACKED_ROWS * capacity
        + to_row % capacity
    )
    reorder[...] = (from_row == origin).astype(jnp.float32).astype(jnp.bfloat16)

    all_slots.wait_recv()
    pass_copy.start()
    pass_copy.wait_recv()
    arrived = slots_in[...].reshape(sources * PACKED_ROWS, width)
    for i in range(fold):
        tokens[:, i * width : (i + 1) * width] = jnp.dot(
            select[i], arrived, preferred_element_type=jnp.float32
        ).astype(jnp.bfloat16)

    tile = fold * LANES

    def hidden_body(step, carry):
        slot = step % hidden_slots
        for copy in hidden_copies(step, slot):
            copy.wait()
        for start in range(0, hidden_step, tile):
            gate_value = jnp.dot(
                tokens[...],
                hidden_weights[slot, 0, :, start : start + tile],
                preferred_element_type=jnp.float32,
            )
            up_value = jnp.dot(
                tokens[...],
                hidden_weights[slot, 1, :, start : start + tile],
                preferred_element_type=jnp.float32,
            )
            value = gate_value / (1.0 + jnp.exp(-gate_value)) * up_value
            where = pl.ds(pl.multiple_of(step * hidden_step + start, tile), tile)
            activated[:, where] = value.astype(jnp.bfloat16)

        @pl.when(step + hidden_slots < hidden_steps)
        def _():
            for copy in hidden_copies(step + hidden_slots, slot):
                copy.start()

        return carry

    lax.fori_loop(0, hidden_steps, hidden_body, 0)

    def half_copy(step):
        return pltpu.make_async_remote_copy(
            src_ref=half_out.at[step],
            dst_ref=half_in.at[step],
            send_sem=half_out_sem.at[step],
            recv_sem=half_in_sem.at[step],
            device_id=sibling,
            device_id_type=MESH,
        )

    def back_copy(step, distance):
        return pltpu.make_async_remote_copy(
            src_ref=back_out.at[step, after(distance)],
            dst_ref=back_in.at[step, me],
            send_sem=back_out_sem.at[step],
            recv_sem=back_in_sem.at[step],
            device_id=holder(after(distance)),
            device_id_type=MESH,
        )

    def all_back(step):
        return pltpu.make_async_remote_copy(
            src_ref=back_out.at[step, others],
            dst_ref=back_in.at[step, others],
            send_sem=back_out_sem.at[step],
            recv_sem=back_in_sem.at[step],
            device_id=sibling,
            device_id_type=MESH,
        )

    def send_back(step):
        half_copy(step).wait_recv()
        total = partial_ref[step, core] + half_in[step].astype(jnp.float32)
        stacked = jnp.concatenate(
            [total[:, i * span : (i + 1) * span] for i in range(fold)], axis=0
        ).astype(jnp.bfloat16)
        ordered = jnp.dot(reorder[...], stacked, preferred_element_type=jnp.float32)
        back_out[step] = ordered.astype(jnp.bfloat16).reshape(experts, PACKED_ROWS, span)
        for distance in range(1, experts):
            back_copy(step, distance).start()
        back_in[step, me] = back_out[step, me]

    def down_body(step, carry):
        for i in range(chunk_steps):
            piece = step * chunk_steps + i
            slot = piece % down_slots
            down_copy(piece, slot).wait()
            produced = jnp.dot(
                activated[...], down_weights[slot], preferred_element_type=jnp.float32
            )
            partial_ref[step, :, :, i * down_step : (i + 1) * down_step] = produced.reshape(
                2, half_rows, down_step
            )

            @pl.when(piece + down_slots < down_steps)
            def _():
                down_copy(piece + down_slots, slot).start()

            if i == 0:

                @pl.when(step > 0)
                def _():
                    send_back(step - 1)

        half_out[step] = partial_ref[step, 1 - core].astype(jnp.bfloat16)
        half_copy(step).start()
        return carry

    lax.fori_loop(0, chunks, down_body, 0)

    def combine(step):
        all_back(step).wait_recv()
        mixed = jnp.dot(
            share_ref[...],
            back_in[step].reshape(packed, span).astype(jnp.float32),
            precision=lax.Precision.HIGHEST,
            preferred_element_type=jnp.float32,
        )
        for i in range(fold):
            where = slice(step * chunk + i * span, step * chunk + (i + 1) * span)
            out_ref[:, where] = (
                hidden_ref[:, where] + mixed[i * rows : (i + 1) * rows]
            ).astype(jnp.bfloat16)

    for step in range(chunks - 2):
        combine(step)
    send_back(chunks - 1)
    for step in range(max(0, chunks - 2), chunks):
        combine(step)

    for copy in attn_copies + [all_slots, pass_copy]:
        copy.wait_send()
    for step in range(chunks):
        half_copy(step).wait_send()
        all_back(step).wait_send()


def fused_shards(resid, attn_part, norm_gain, w_router, routes, w_gate, w_up, w_down):
    tensor_ranks = lax.axis_size("tensor")
    rows, features = resid.shape
    capacity = rows // 2
    fold = PACKED_ROWS // capacity
    width = features // fold
    hidden_units = w_gate.shape[1]
    step = fold * LANES
    hidden_step = 2 * step if hidden_units % (2 * step) == 0 else step
    hidden_steps, down_steps = hidden_units // hidden_step, features // step
    down_slots = min(down_steps, 4)
    chunk = 2 * step if down_steps % 2 == 0 else step
    chunks = features // chunk
    hidden_bytes, down_bytes = 4 * features * hidden_step, 2 * hidden_units * step
    hidden_slots = min(hidden_steps, (WEIGHT_BYTES - down_slots * down_bytes) // hidden_bytes)
    dma = pltpu.SemaphoreType.DMA
    bf16, f32 = jnp.bfloat16, jnp.float32
    half_rows = E * capacity
    weights = 2 * features * hidden_units + hidden_units * features
    return pl.pallas_call(
        functools.partial(fused_kernel, (E, tensor_ranks, capacity, hidden_slots, down_slots)),
        out_shape=jax.ShapeDtypeStruct(resid.shape, bf16),
        in_specs=[pl.BlockSpec(memory_space=pl.ANY)] * 8,
        out_specs=pl.BlockSpec(memory_space=pltpu.VMEM),
        scratch_shapes=[
            pltpu.VMEM(resid.shape, bf16),
            pltpu.VMEM(attn_part.shape, bf16),
            pltpu.VMEM((1, features), f32),
            pltpu.VMEM(w_router.shape[::-1], bf16),
            pltpu.VMEM(routes.shape[::-1], jnp.int32),
            dma((5,)),
            pltpu.VMEM((hidden_slots, 2, features, hidden_step), bf16),
            dma((hidden_slots, 2)),
            pltpu.VMEM((down_slots, hidden_units, step), bf16),
            dma((down_slots,)),
            pltpu.VMEM((tensor_ranks, 2 * rows, features // 2), bf16),
            pltpu.VMEM((tensor_ranks - 1, 2 * rows, features // 2), bf16),
            dma((tensor_ranks - 1,)),
            dma((tensor_ranks - 1,)),
            pltpu.VMEM(resid.shape, f32),
            pltpu.VMEM((fold * rows, E * PACKED_ROWS), f32),
            pltpu.VMEM((E, PACKED_ROWS, width), bf16),
            pltpu.VMEM((2, E, PACKED_ROWS, width), bf16),
            dma(()),
            dma(()),
            dma(()),
            dma(()),
            pltpu.VMEM((fold, 2 * half_rows, 2 * E * PACKED_ROWS), bf16),
            pltpu.VMEM((E * PACKED_ROWS, E * PACKED_ROWS), bf16),
            pltpu.VMEM((2 * half_rows, features), bf16),
            pltpu.VMEM((2 * half_rows, hidden_units), bf16),
            pltpu.VMEM((chunks, 2, half_rows, chunk), f32),
            pltpu.VMEM((chunks, half_rows, chunk), bf16),
            pltpu.VMEM((chunks, half_rows, chunk), bf16),
            dma((chunks,)),
            dma((chunks,)),
            pltpu.VMEM((chunks, E, PACKED_ROWS, chunk // fold), bf16),
            pltpu.VMEM((chunks, E, PACKED_ROWS, chunk // fold), bf16),
            dma((chunks,)),
            dma((chunks,)),
        ],
        compiler_params=pltpu.CompilerParams(
            collective_id=0, has_side_effects=True, vmem_limit_bytes=VMEM_BYTES
        ),
        cost_estimate=pl.CostEstimate(
            flops=2 * 2 * half_rows * weights,
            bytes_accessed=2 * weights,
            transcendentals=2 * half_rows * hidden_units,
        ),
    )(resid, attn_part, norm_gain.reshape(1, features), w_router.T, routes.T, w_gate, w_up, w_down)


def fits(mesh):
    ranks = mesh.shape["expert"] * mesh.shape["tensor"]
    return ranks == 2 * E and mesh.shape["tensor"] % 2 == 0


def solution(mesh):
    return jax.shard_map(
        fused_shards if fits(mesh) else shards,
        mesh=mesh,
        in_specs=(
            P(("groups", "expert", "tensor"), None),
            P(("groups", "expert"), "tensor"),
            P(),
            P(),
            P(("groups", "expert", "tensor"), None),
            P(None, ("expert", "tensor")),
            P(None, ("expert", "tensor")),
            P(("expert", "tensor"), None),
        ),
        out_specs=P(("groups", "expert", "tensor"), None),
        check_vma=False,
    )
```

```python
import functools

import jax
import jax.numpy as jnp
from jax import lax
from jax.experimental import pallas as pl
from jax.experimental.pallas import tpu as pltpu
from jax.sharding import PartitionSpec as P

E = 8
MESH = pl.DeviceIdType.MESH


EPSILON = 1e-05


def partner(shard, axis, distance):
    return lax.ppermute(shard, axis, [(i, i ^ 1 << distance) for i in range(lax.axis_size(axis))])


def shards(resid, attn_part, norm_gain, w_router, routes, w_gate, w_up, w_down):
    expert_ranks = lax.axis_size("expert")
    tensor_ranks = lax.axis_size("tensor")
    my_expert_rank = lax.axis_index("expert")
    my_tensor_rank = lax.axis_index("tensor")
    token_rows = resid.shape[0]
    feature_count = resid.shape[1]
    holders = max(1, expert_ranks // E)
    hosted = max(1, E // expert_ranks)
    expert_groups = E // hosted
    capacity = token_rows // 2
    rank_slots = hosted * capacity
    feature_share = feature_count // holders
    levels = holders.bit_length() - 1
    partial_terms = attn_part.astype(jnp.float32)
    attn_rows = lax.psum_scatter(
        partial_terms.astype(jnp.bfloat16), "tensor", scatter_dimension=0, tiled=True
    ).astype(jnp.float32)
    hidden_state = (resid.astype(jnp.float32) + attn_rows).astype(jnp.bfloat16)
    hidden_wide = lax.optimization_barrier(hidden_state).astype(jnp.float32)
    inverse_rms = lax.rsqrt(jnp.mean(hidden_wide * hidden_wide, axis=1, keepdims=True) + EPSILON)
    normed = (hidden_wide * inverse_rms * norm_gain).astype(jnp.bfloat16)
    logits = jnp.dot(normed, w_router, preferred_element_type=jnp.float32)
    expert_columns = lax.broadcasted_iota(jnp.int32, (token_rows, E), 1)
    pick_first = (routes[:, 0:1] == expert_columns).astype(jnp.float32)
    pick_second = (routes[:, 1:2] == expert_columns).astype(jnp.float32)
    share_first = jax.nn.sigmoid(jnp.sum((pick_first - pick_second) * logits, axis=1))
    share_second = 1.0 - share_first
    row_later = lax.broadcasted_iota(jnp.int32, (token_rows, token_rows), 0)
    row_earlier = lax.broadcasted_iota(jnp.int32, (token_rows, token_rows), 1)
    earlier = (row_later > row_earlier).astype(jnp.float32)
    before = jnp.dot(earlier, pick_first + pick_second, precision=lax.Precision.HIGHEST)
    slot_first = jnp.sum(before * pick_first, axis=1)
    slot_second = jnp.sum(before * pick_second, axis=1)
    slot_numbers = lax.broadcasted_iota(jnp.int32, (token_rows, E, capacity), 2).astype(jnp.float32)
    cell_first = pick_first[:, :, None] * (slot_numbers == slot_first[:, None, None]).astype(
        jnp.float32
    )
    cell_second = pick_second[:, :, None] * (slot_numbers == slot_second[:, None, None]).astype(
        jnp.float32
    )
    placement = (
        (cell_first + cell_second)
        .reshape(token_rows, expert_groups, rank_slots)
        .astype(jnp.bfloat16)
    )
    combine_weight = (
        share_first[:, None, None] * cell_first + share_second[:, None, None] * cell_second
    ).reshape(token_rows, expert_groups, rank_slots)
    outgoing = jnp.einsum(
        "rgc,rd->gcd", placement, normed, preferred_element_type=jnp.float32
    ).astype(jnp.bfloat16)
    outgoing = jnp.repeat(outgoing, holders, axis=0)
    arrived = lax.all_to_all(outgoing, "expert", split_axis=0, concat_axis=0, tiled=True)
    device_span = my_expert_rank * tensor_ranks + my_tensor_rank
    own_expert = device_span * E // (expert_ranks * tensor_ranks)
    local_index = own_expert - my_expert_rank // holders * hosted

    def activate(token_block):
        source_count = token_block.shape[0]
        selected = lax.dynamic_slice_in_dim(token_block, local_index * capacity, capacity, 1)
        flattened = selected.reshape(source_count * capacity, feature_count)
        gate_value = jnp.dot(flattened, w_gate, preferred_element_type=jnp.float32)
        up_value = jnp.dot(flattened, w_up, preferred_element_type=jnp.float32)
        return (jax.nn.silu(gate_value) * up_value).astype(jnp.bfloat16)

    def expert_partial(token_block):
        source_count = token_block.shape[0]
        activated = activate(token_block)
        produced = jnp.dot(activated, w_down, preferred_element_type=jnp.float32).reshape(
            source_count, capacity, feature_count
        )
        if hosted == 1:
            return produced
        blank = jnp.zeros((source_count, rank_slots, feature_count), jnp.float32)
        return lax.dynamic_update_slice_in_dim(blank, produced, local_index * capacity, 1)

    partial_value = expert_partial(lax.all_gather(arrived, "tensor", axis=0, tiled=True))
    leading = partial_value.shape[0]
    layered = partial_value.reshape((leading, rank_slots) + (2,) * levels + (feature_share,))
    remaining = [section for section in range(levels - 1, -1, -1)]
    for section in range(levels):
        split_axis = 2 + remaining.index(section)
        my_side = my_expert_rank // 2**section % 2
        kept_half = lax.dynamic_index_in_dim(layered, my_side, split_axis, keepdims=False)
        given_half = lax.dynamic_index_in_dim(layered, 1 - my_side, split_axis, keepdims=False)
        layered = kept_half + partner(given_half.astype(jnp.bfloat16), "expert", section).astype(
            given_half.dtype
        )
        remaining = [other for other in remaining if other != section]
    own_sources = lax.psum_scatter(
        layered.astype(jnp.bfloat16), "tensor", scatter_dimension=0, tiled=True
    ).astype(jnp.float32)
    returned = lax.all_to_all(
        own_sources.astype(jnp.bfloat16), "expert", split_axis=0, concat_axis=0, tiled=True
    ).astype(own_sources.dtype)
    returned_view = returned.reshape(expert_groups, holders, rank_slots, feature_share)
    mixed = jnp.einsum(
        "rgc,gscp->rsp", combine_weight, returned_view, precision=lax.Precision.HIGHEST
    )
    mixed = mixed.reshape(token_rows, feature_count)
    return (hidden_wide + mixed).astype(jnp.bfloat16)


LANES = 128
PACKED_ROWS = 16
WEIGHT_BYTES = 52 << 20
VMEM_BYTES = 60 << 20


def log(power):
    return power.bit_length() - 1


def fused_kernel(
    sizes,
    resid_hbm,
    attn_hbm,
    gain_hbm,
    router_hbm,
    routes_hbm,
    gate_hbm,
    up_hbm,
    down_hbm,
    out_ref,
    resid,
    attn,
    gain,
    router,
    routes,
    in_sem,
    hidden_weights,
    hidden_sem,
    down_weights,
    down_sem,
    attn_out,
    attn_in,
    attn_out_sem,
    attn_in_sem,
    hidden_ref,
    share_ref,
    slots_out,
    slots_in,
    slots_out_sem,
    slots_in_sem,
    pass_out_sem,
    pass_in_sem,
    select,
    reorder,
    tokens,
    activated,
    partial_ref,
    half_out,
    half_in,
    half_out_sem,
    half_in_sem,
    back_out,
    back_in,
    back_out_sem,
    back_in_sem,
):
    experts, tensor_ranks, capacity, hidden_slots, down_slots = sizes
    rows, features = resid.shape
    fold = PACKED_ROWS // capacity
    width = features // fold
    hidden_step = hidden_weights.shape[3]
    hidden_steps = gate_hbm.shape[1] // hidden_step
    down_step = down_weights.shape[2]
    chunks, _, _, chunk = partial_ref.shape
    chunk_steps = chunk // down_step
    down_steps = chunks * chunk_steps
    span = chunk // fold
    pairs = tensor_ranks // 2
    group = lax.axis_index("groups")
    my_z = lax.axis_index("expert")
    my_t = lax.axis_index("tensor")
    core = lax.rem(my_t, 2)
    me = my_z * pairs + lax.div(my_t, 2)
    sibling = (group, my_z, my_t + 1 - 2 * core)

    after = [lax.rem(me + step, experts) for step in range(experts)]
    holder = [
        (group, lax.div(number, pairs), lax.rem(number, pairs) * 2 + core) for number in after
    ]
    tensor_after = [lax.rem(my_t + step, tensor_ranks) for step in range(tensor_ranks)]

    small = [
        pltpu.make_async_copy(source, target, in_sem.at[i])
        for i, (source, target) in enumerate(
            (
                (attn_hbm, attn),
                (resid_hbm, resid),
                (gain_hbm, gain),
                (router_hbm, router),
                (routes_hbm, routes),
            )
        )
    ]
    for copy in small:
        copy.start()

    barrier = pltpu.get_barrier_semaphore()
    tensor_peers = [(group, my_z, tensor_after[i]) for i in range(1, tensor_ranks, 2)]
    peers = holder[1:]
    for peer in tensor_peers + peers:
        pl.semaphore_signal(barrier, inc=1, device_id=peer, device_id_type=MESH)

    def hidden_copies(step, slot):
        columns = pl.ds(pl.multiple_of(step * hidden_step, hidden_step), hidden_step)
        return [
            pltpu.make_async_copy(
                source.at[:, columns], hidden_weights.at[slot, i], hidden_sem.at[slot, i]
            )
            for i, source in enumerate((gate_hbm, up_hbm))
        ]

    def down_copy(step, slot):
        columns = pl.ds(pl.multiple_of(step * down_step, down_step), down_step)
        return pltpu.make_async_copy(
            down_hbm.at[:, columns], down_weights.at[slot], down_sem.at[slot]
        )

    def start_hidden(step):
        for copy in hidden_copies(step, step):
            copy.start()

    start_hidden(0)
    small[0].wait()
    terms = attn[...].astype(jnp.float32)
    half = features // 2
    for i in range(tensor_ranks):
        block = terms[i * rows : (i + 1) * rows]
        attn_out[i] = jnp.concatenate([block[:, :half], block[:, half:]], axis=0).astype(
            jnp.bfloat16
        )
    pl.semaphore_wait(barrier, len(tensor_peers) + len(peers))

    def attn_copy(step):
        target = tensor_after[step]
        return pltpu.make_async_remote_copy(
            src_ref=attn_out.at[target],
            dst_ref=attn_in.at[step - 1],
            send_sem=attn_out_sem.at[step - 1],
            recv_sem=attn_in_sem.at[step - 1],
            device_id=(group, my_z, target),
            device_id_type=MESH,
        )

    attn_copies = [attn_copy(step) for step in range(1, tensor_ranks)]
    for copy in attn_copies:
        copy.start()
    for step in range(1, min(2, hidden_slots)):
        start_hidden(step)
    for copy in small[1:]:
        copy.wait()
    diagonal = lax.broadcasted_iota(jnp.int32, (rows, rows), 0) == lax.broadcasted_iota(
        jnp.int32, (rows, rows), 1
    )
    first, second = [
        jnp.sum(jnp.where(diagonal, routes[i : i + 1].astype(jnp.float32), 0.0), axis=1, keepdims=True)
        .astype(jnp.int32)
        for i in range(2)
    ]
    columns = lax.broadcasted_iota(jnp.int32, (rows, LANES), 1)
    row_number = lax.broadcasted_iota(jnp.int32, (rows, LANES), 0)
    pick_first = (columns == first).astype(jnp.float32)
    pick_second = (columns == second).astype(jnp.float32)
    both = pick_first + pick_second
    earlier = jnp.zeros((rows, LANES), jnp.float32)
    for i in range(rows):
        earlier += jnp.where(row_number > i, both[i : i + 1], 0.0)
    slot_first = jnp.sum(earlier * pick_first, axis=1, keepdims=True).astype(jnp.int32)
    slot_second = jnp.sum(earlier * pick_second, axis=1, keepdims=True).astype(jnp.int32)
    place_first = jnp.concatenate([first * PACKED_ROWS + slot_first] * fold, axis=0)
    place_second = jnp.concatenate([second * PACKED_ROWS + slot_second] * fold, axis=0)
    packed = experts * PACKED_ROWS
    part = lax.broadcasted_iota(jnp.int32, (fold * rows, packed), 0)
    part = (part >> log(rows)) * capacity
    cells = lax.broadcasted_iota(jnp.int32, (fold * rows, packed), 1) - part
    cell_first = (cells == place_first).astype(jnp.float32)
    cell_second = (cells == place_second).astype(jnp.float32)
    placement = (cell_first + cell_second).T.astype(jnp.bfloat16)

    summed = attn_out[my_t].astype(jnp.float32)
    for i, copy in enumerate(attn_copies):
        copy.wait_recv()
        summed += attn_in[i].astype(jnp.float32)
    attn_sum = jnp.concatenate([summed[:rows], summed[rows:]], axis=1)
    hidden_wide = (
        (resid[...].astype(jnp.float32) + attn_sum).astype(jnp.bfloat16).astype(jnp.float32)
    )
    hidden_ref[...] = hidden_wide
    mean_square = jnp.sum(hidden_wide * hidden_wide, axis=1, keepdims=True) / features
    normed_wide = hidden_wide * lax.rsqrt(mean_square + EPSILON) * gain[...]
    normed = normed_wide.astype(jnp.bfloat16)
    folded = jnp.concatenate(
        [normed_wide[:, i * width : (i + 1) * width] for i in range(fold)], axis=0
    ).astype(jnp.bfloat16)
    outgoing = jnp.dot(placement, folded, preferred_element_type=jnp.float32)
    slots_out[...] = outgoing.astype(jnp.bfloat16).reshape(experts, PACKED_ROWS, width)

    def slot_copy(step):
        return pltpu.make_async_remote_copy(
            src_ref=slots_out.at[after[step]],
            dst_ref=slots_in.at[core, me],
            send_sem=slots_out_sem,
            recv_sem=slots_in_sem,
            device_id=holder[step],
            device_id_type=MESH,
        )

    others = pl.ds(0, experts - 1)
    all_slots = pltpu.make_async_remote_copy(
        src_ref=slots_out.at[others],
        dst_ref=slots_in.at[core, others],
        send_sem=slots_out_sem,
        recv_sem=slots_in_sem,
        device_id=sibling,
        device_id_type=MESH,
    )
    pass_copy = pltpu.make_async_remote_copy(
        src_ref=slots_in.at[core],
        dst_ref=slots_in.at[core],
        send_sem=pass_out_sem,
        recv_sem=pass_in_sem,
        device_id=sibling,
        device_id_type=MESH,
    )
    for step in sorted(range(1, experts), key=lambda step: abs(2 * step - experts - 1)):
        slot_copy(step).start()
    for step in range(2, hidden_slots):
        start_hidden(step)
    for step in range(down_slots):
        down_copy(step, step).start()
    slots_in[core, me] = slots_out[me]

    logits = lax.dot_general(
        normed, router[...], (((1,), (1,)), ((), ())), preferred_element_type=jnp.float32
    )
    expert_columns = lax.broadcasted_iota(jnp.int32, (rows, experts), 1)
    logit_first = jnp.sum(jnp.where(expert_columns == first, logits, 0.0), axis=1, keepdims=True)
    logit_second = jnp.sum(jnp.where(expert_columns == second, logits, 0.0), axis=1, keepdims=True)
    share_first = 1.0 / (1.0 + jnp.exp(logit_second - logit_first))
    share_second = 1.0 - share_first
    share = (
        jnp.concatenate([share_first] * fold, axis=0) * cell_first
        + jnp.concatenate([share_second] * fold, axis=0) * cell_second
    )
    for i in range(3):
        term = share.astype(jnp.bfloat16)
        share_ref[i * fold * rows : (i + 1) * fold * rows] = term
        share = share - term.astype(jnp.float32)

    sources = 2 * experts
    token_rows = sources * capacity
    token_number = lax.broadcasted_iota(jnp.int32, (token_rows, sources * PACKED_ROWS), 0)
    packed_number = lax.broadcasted_iota(jnp.int32, (token_rows, sources * PACKED_ROWS), 1)
    wanted = (token_number >> log(capacity)) * PACKED_ROWS + (token_number & (capacity - 1))
    for i in range(fold):
        select[i] = (
            (packed_number == wanted + i * capacity).astype(jnp.float32).astype(jnp.bfloat16)
        )
    half_rows = experts * capacity
    to_row = lax.broadcasted_iota(jnp.int32, (packed, packed), 0)
    from_row = lax.broadcasted_iota(jnp.int32, (packed, packed), 1)
    origin = (
        ((to_row & (PACKED_ROWS - 1)) >> log(capacity)) * half_rows
        + (to_row >> log(PACKED_ROWS)) * capacity
        + (to_row & (capacity - 1))
    )
    reorder[...] = (from_row == origin).astype(jnp.float32).astype(jnp.bfloat16)

    all_slots.wait_recv()
    pass_copy.start()
    pass_copy.wait_recv()
    arrived = slots_in[...].reshape(sources * PACKED_ROWS, width)
    for i in range(fold):
        tokens[:, i * width : (i + 1) * width] = jnp.dot(
            select[i], arrived, preferred_element_type=jnp.float32
        ).astype(jnp.bfloat16)

    tile = fold * LANES

    def hidden_body(step, carry):
        slot = step % hidden_slots
        for copy in hidden_copies(step, slot):
            copy.wait()
        for start in range(0, hidden_step, tile):
            gate_value = jnp.dot(
                tokens[...],
                hidden_weights[slot, 0, :, start : start + tile],
                preferred_element_type=jnp.float32,
            )
            up_value = jnp.dot(
                tokens[...],
                hidden_weights[slot, 1, :, start : start + tile],
                preferred_element_type=jnp.float32,
            )
            value = gate_value / (1.0 + jnp.exp(-gate_value)) * up_value
            where = pl.ds(pl.multiple_of(step * hidden_step + start, tile), tile)
            activated[:, where] = value.astype(jnp.bfloat16)

        @pl.when(step + hidden_slots < hidden_steps)
        def _():
            for copy in hidden_copies(step + hidden_slots, slot):
                copy.start()

        return carry

    lax.fori_loop(0, hidden_steps, hidden_body, 0)

    def half_copy(step):
        return pltpu.make_async_remote_copy(
            src_ref=half_out.at[step],
            dst_ref=half_in.at[step],
            send_sem=half_out_sem.at[step],
            recv_sem=half_in_sem.at[step],
            device_id=sibling,
            device_id_type=MESH,
        )

    def back_copy(step, distance):
        return pltpu.make_async_remote_copy(
            src_ref=back_out.at[step, after[distance]],
            dst_ref=back_in.at[step, me],
            send_sem=back_out_sem.at[step],
            recv_sem=back_in_sem.at[step],
            device_id=holder[distance],
            device_id_type=MESH,
        )

    def all_back(step):
        return pltpu.make_async_remote_copy(
            src_ref=back_out.at[step, others],
            dst_ref=back_in.at[step, others],
            send_sem=back_out_sem.at[step],
            recv_sem=back_in_sem.at[step],
            device_id=sibling,
            device_id_type=MESH,
        )

    def send_back(step):
        half_copy(step).wait_recv()
        total = partial_ref[step, core] + half_in[step].astype(jnp.float32)
        stacked = jnp.concatenate(
            [total[:, i * span : (i + 1) * span] for i in range(fold)], axis=0
        ).astype(jnp.bfloat16)
        ordered = jnp.dot(reorder[...], stacked, preferred_element_type=jnp.float32)
        back_out[step] = ordered.astype(jnp.bfloat16).reshape(experts, PACKED_ROWS, span)
        for distance in range(1, experts):
            back_copy(step, distance).start()
        back_in[step, me] = back_out[step, me]

    def down_body(step, carry):
        for i in range(chunk_steps):
            piece = step * chunk_steps + i
            slot = piece % down_slots
            down_copy(piece, slot).wait()
            produced = jnp.dot(
                activated[...], down_weights[slot], preferred_element_type=jnp.float32
            )
            partial_ref[step, :, :, i * down_step : (i + 1) * down_step] = produced.reshape(
                2, half_rows, down_step
            )

            @pl.when(piece + down_slots < down_steps)
            def _():
                down_copy(piece + down_slots, slot).start()

            if i == 0:

                @pl.when(step > 0)
                def _():
                    send_back(step - 1)

        half_out[step] = partial_ref[step, 1 - core].astype(jnp.bfloat16)
        half_copy(step).start()
        return carry

    lax.fori_loop(0, chunks, down_body, 0)

    def combine(step):
        all_back(step).wait_recv()
        mixed = jnp.dot(
            share_ref[...],
            back_in[step].reshape(packed, span),
            preferred_element_type=jnp.float32,
        )
        terms = fold * rows
        mixed = mixed[:terms] + (mixed[terms : 2 * terms] + mixed[2 * terms :])
        for i in range(fold):
            where = slice(step * chunk + i * span, step * chunk + (i + 1) * span)
            out_ref[:, where] = (
                hidden_ref[:, where] + mixed[i * rows : (i + 1) * rows]
            ).astype(jnp.bfloat16)

    for step in range(chunks - 2):
        combine(step)
    send_back(chunks - 1)
    for step in range(max(0, chunks - 2), chunks):
        combine(step)

    for copy in attn_copies + [all_slots, pass_copy]:
        copy.wait_send()
    for step in range(chunks):
        half_copy(step).wait_send()
        all_back(step).wait_send()


def fused_shards(resid, attn_part, norm_gain, w_router, routes, w_gate, w_up, w_down):
    tensor_ranks = lax.axis_size("tensor")
    rows, features = resid.shape
    capacity = rows // 2
    fold = PACKED_ROWS // capacity
    width = features // fold
    hidden_units = w_gate.shape[1]
    step = fold * LANES
    hidden_step = 2 * step if hidden_units % (2 * step) == 0 else step
    hidden_steps, down_steps = hidden_units // hidden_step, features // step
    down_slots = min(down_steps, 4)
    chunk = 2 * step if down_steps % 2 == 0 else step
    chunks = features // chunk
    hidden_bytes, down_bytes = 4 * features * hidden_step, 2 * hidden_units * step
    hidden_slots = min(hidden_steps, (WEIGHT_BYTES - down_slots * down_bytes) // hidden_bytes)
    dma = pltpu.SemaphoreType.DMA
    bf16, f32 = jnp.bfloat16, jnp.float32
    half_rows = E * capacity
    weights = 2 * features * hidden_units + hidden_units * features
    return pl.pallas_call(
        functools.partial(fused_kernel, (E, tensor_ranks, capacity, hidden_slots, down_slots)),
        out_shape=jax.ShapeDtypeStruct(resid.shape, bf16),
        in_specs=[pl.BlockSpec(memory_space=pl.ANY)] * 8,
        out_specs=pl.BlockSpec(memory_space=pltpu.VMEM),
        scratch_shapes=[
            pltpu.VMEM(resid.shape, bf16),
            pltpu.VMEM(attn_part.shape, bf16),
            pltpu.VMEM((1, features), f32),
            pltpu.VMEM(w_router.shape[::-1], bf16),
            pltpu.VMEM(routes.shape[::-1], jnp.int32),
            dma((5,)),
            pltpu.VMEM((hidden_slots, 2, features, hidden_step), bf16),
            dma((hidden_slots, 2)),
            pltpu.VMEM((down_slots, hidden_units, step), bf16),
            dma((down_slots,)),
            pltpu.VMEM((tensor_ranks, 2 * rows, features // 2), bf16),
            pltpu.VMEM((tensor_ranks - 1, 2 * rows, features // 2), bf16),
            dma((tensor_ranks - 1,)),
            dma((tensor_ranks - 1,)),
            pltpu.VMEM(resid.shape, f32),
            pltpu.VMEM((3 * fold * rows, E * PACKED_ROWS), bf16),
            pltpu.VMEM((E, PACKED_ROWS, width), bf16),
            pltpu.VMEM((2, E, PACKED_ROWS, width), bf16),
            dma(()),
            dma(()),
            dma(()),
            dma(()),
            pltpu.VMEM((fold, 2 * half_rows, 2 * E * PACKED_ROWS), bf16),
            pltpu.VMEM((E * PACKED_ROWS, E * PACKED_ROWS), bf16),
            pltpu.VMEM((2 * half_rows, features), bf16),
            pltpu.VMEM((2 * half_rows, hidden_units), bf16),
            pltpu.VMEM((chunks, 2, half_rows, chunk), f32),
            pltpu.VMEM((chunks, half_rows, chunk), bf16),
            pltpu.VMEM((chunks, half_rows, chunk), bf16),
            dma((chunks,)),
            dma((chunks,)),
            pltpu.VMEM((chunks, E, PACKED_ROWS, chunk // fold), bf16),
            pltpu.VMEM((chunks, E, PACKED_ROWS, chunk // fold), bf16),
            dma((chunks,)),
            dma((chunks,)),
        ],
        compiler_params=pltpu.CompilerParams(
            collective_id=0, has_side_effects=True, vmem_limit_bytes=VMEM_BYTES
        ),
        cost_estimate=pl.CostEstimate(
            flops=2 * 2 * half_rows * weights,
            bytes_accessed=2 * weights,
            transcendentals=2 * half_rows * hidden_units,
        ),
    )(resid, attn_part, norm_gain.reshape(1, features), w_router.T, routes.T, w_gate, w_up, w_down)


def fits(mesh):
    ranks = mesh.shape["expert"] * mesh.shape["tensor"]
    return ranks == 2 * E and mesh.shape["tensor"] % 2 == 0


def solution(mesh):
    return jax.shard_map(
        fused_shards if fits(mesh) else shards,
        mesh=mesh,
        in_specs=(
            P(("groups", "expert", "tensor"), None),
            P(("groups", "expert"), "tensor"),
            P(),
            P(),
            P(("groups", "expert", "tensor"), None),
            P(None, ("expert", "tensor")),
            P(None, ("expert", "tensor")),
            P(("expert", "tensor"), None),
        ),
        out_specs=P(("groups", "expert", "tensor"), None),
        check_vma=False,
    )
```

```python
import functools

import jax
import jax.numpy as jnp
from jax import lax
from jax.experimental import pallas as pl
from jax.experimental.pallas import tpu as pltpu
from jax.sharding import PartitionSpec as P

E = 8
MESH = pl.DeviceIdType.MESH


EPSILON = 1e-05


def partner(shard, axis, distance):
    return lax.ppermute(shard, axis, [(i, i ^ 1 << distance) for i in range(lax.axis_size(axis))])


def shards(resid, attn_part, norm_gain, w_router, routes, w_gate, w_up, w_down):
    expert_ranks = lax.axis_size("expert")
    tensor_ranks = lax.axis_size("tensor")
    my_expert_rank = lax.axis_index("expert")
    my_tensor_rank = lax.axis_index("tensor")
    token_rows = resid.shape[0]
    feature_count = resid.shape[1]
    holders = max(1, expert_ranks // E)
    hosted = max(1, E // expert_ranks)
    expert_groups = E // hosted
    capacity = token_rows // 2
    rank_slots = hosted * capacity
    feature_share = feature_count // holders
    levels = holders.bit_length() - 1
    partial_terms = attn_part.astype(jnp.float32)
    attn_rows = lax.psum_scatter(
        partial_terms.astype(jnp.bfloat16), "tensor", scatter_dimension=0, tiled=True
    ).astype(jnp.float32)
    hidden_state = (resid.astype(jnp.float32) + attn_rows).astype(jnp.bfloat16)
    hidden_wide = lax.optimization_barrier(hidden_state).astype(jnp.float32)
    inverse_rms = lax.rsqrt(jnp.mean(hidden_wide * hidden_wide, axis=1, keepdims=True) + EPSILON)
    normed = (hidden_wide * inverse_rms * norm_gain).astype(jnp.bfloat16)
    logits = jnp.dot(normed, w_router, preferred_element_type=jnp.float32)
    expert_columns = lax.broadcasted_iota(jnp.int32, (token_rows, E), 1)
    pick_first = (routes[:, 0:1] == expert_columns).astype(jnp.float32)
    pick_second = (routes[:, 1:2] == expert_columns).astype(jnp.float32)
    share_first = jax.nn.sigmoid(jnp.sum((pick_first - pick_second) * logits, axis=1))
    share_second = 1.0 - share_first
    row_later = lax.broadcasted_iota(jnp.int32, (token_rows, token_rows), 0)
    row_earlier = lax.broadcasted_iota(jnp.int32, (token_rows, token_rows), 1)
    earlier = (row_later > row_earlier).astype(jnp.float32)
    before = jnp.dot(earlier, pick_first + pick_second, precision=lax.Precision.HIGHEST)
    slot_first = jnp.sum(before * pick_first, axis=1)
    slot_second = jnp.sum(before * pick_second, axis=1)
    slot_numbers = lax.broadcasted_iota(jnp.int32, (token_rows, E, capacity), 2).astype(jnp.float32)
    cell_first = pick_first[:, :, None] * (slot_numbers == slot_first[:, None, None]).astype(
        jnp.float32
    )
    cell_second = pick_second[:, :, None] * (slot_numbers == slot_second[:, None, None]).astype(
        jnp.float32
    )
    placement = (
        (cell_first + cell_second)
        .reshape(token_rows, expert_groups, rank_slots)
        .astype(jnp.bfloat16)
    )
    combine_weight = (
        share_first[:, None, None] * cell_first + share_second[:, None, None] * cell_second
    ).reshape(token_rows, expert_groups, rank_slots)
    outgoing = jnp.einsum(
        "rgc,rd->gcd", placement, normed, preferred_element_type=jnp.float32
    ).astype(jnp.bfloat16)
    outgoing = jnp.repeat(outgoing, holders, axis=0)
    arrived = lax.all_to_all(outgoing, "expert", split_axis=0, concat_axis=0, tiled=True)
    device_span = my_expert_rank * tensor_ranks + my_tensor_rank
    own_expert = device_span * E // (expert_ranks * tensor_ranks)
    local_index = own_expert - my_expert_rank // holders * hosted

    def activate(token_block):
        source_count = token_block.shape[0]
        selected = lax.dynamic_slice_in_dim(token_block, local_index * capacity, capacity, 1)
        flattened = selected.reshape(source_count * capacity, feature_count)
        gate_value = jnp.dot(flattened, w_gate, preferred_element_type=jnp.float32)
        up_value = jnp.dot(flattened, w_up, preferred_element_type=jnp.float32)
        return (jax.nn.silu(gate_value) * up_value).astype(jnp.bfloat16)

    def expert_partial(token_block):
        source_count = token_block.shape[0]
        activated = activate(token_block)
        produced = jnp.dot(activated, w_down, preferred_element_type=jnp.float32).reshape(
            source_count, capacity, feature_count
        )
        if hosted == 1:
            return produced
        blank = jnp.zeros((source_count, rank_slots, feature_count), jnp.float32)
        return lax.dynamic_update_slice_in_dim(blank, produced, local_index * capacity, 1)

    partial_value = expert_partial(lax.all_gather(arrived, "tensor", axis=0, tiled=True))
    leading = partial_value.shape[0]
    layered = partial_value.reshape((leading, rank_slots) + (2,) * levels + (feature_share,))
    remaining = [section for section in range(levels - 1, -1, -1)]
    for section in range(levels):
        split_axis = 2 + remaining.index(section)
        my_side = my_expert_rank // 2**section % 2
        kept_half = lax.dynamic_index_in_dim(layered, my_side, split_axis, keepdims=False)
        given_half = lax.dynamic_index_in_dim(layered, 1 - my_side, split_axis, keepdims=False)
        layered = kept_half + partner(given_half.astype(jnp.bfloat16), "expert", section).astype(
            given_half.dtype
        )
        remaining = [other for other in remaining if other != section]
    own_sources = lax.psum_scatter(
        layered.astype(jnp.bfloat16), "tensor", scatter_dimension=0, tiled=True
    ).astype(jnp.float32)
    returned = lax.all_to_all(
        own_sources.astype(jnp.bfloat16), "expert", split_axis=0, concat_axis=0, tiled=True
    ).astype(own_sources.dtype)
    returned_view = returned.reshape(expert_groups, holders, rank_slots, feature_share)
    mixed = jnp.einsum(
        "rgc,gscp->rsp", combine_weight, returned_view, precision=lax.Precision.HIGHEST
    )
    mixed = mixed.reshape(token_rows, feature_count)
    return (hidden_wide + mixed).astype(jnp.bfloat16)


LANES = 128
PACKED_ROWS = 16
WEIGHT_BYTES = 52 << 20
VMEM_BYTES = 61 << 20


def log(power):
    return power.bit_length() - 1


def fused_kernel(
    sizes,
    resid_hbm,
    attn_hbm,
    gain_hbm,
    router_hbm,
    routes_hbm,
    gate_hbm,
    up_hbm,
    down_hbm,
    out_ref,
    resid,
    attn,
    gain,
    router,
    routes,
    in_sem,
    hidden_weights,
    hidden_sem,
    down_weights,
    down_sem,
    attn_out,
    attn_in,
    attn_out_sem,
    attn_in_sem,
    hidden_ref,
    share_ref,
    slots_out,
    slots_in,
    slots_out_sem,
    slots_in_sem,
    pass_out_sem,
    pass_in_sem,
    select,
    reorder,
    tokens,
    gate_sum,
    up_sum,
    activated,
    partial_ref,
    half_out,
    half_in,
    half_out_sem,
    half_in_sem,
    back_out,
    back_in,
    back_out_sem,
    back_in_sem,
):
    experts, tensor_ranks, capacity, hidden_slots, down_slots = sizes
    rows, features = resid.shape
    fold = PACKED_ROWS // capacity
    parts = slots_out.shape[0]
    part_features = features // parts
    width = part_features // fold
    hidden_units = gate_hbm.shape[1]
    hidden_step = hidden_weights.shape[2]
    hidden_steps = features // hidden_step
    part_steps = hidden_steps // parts
    down_step = down_weights.shape[2]
    chunks, _, _, chunk = partial_ref.shape
    chunk_steps = chunk // down_step
    down_steps = chunks * chunk_steps
    span = chunk // fold
    pairs = tensor_ranks // 2
    group = lax.axis_index("groups")
    my_z = lax.axis_index("expert")
    my_t = lax.axis_index("tensor")
    core = lax.rem(my_t, 2)
    me = my_z * pairs + lax.div(my_t, 2)
    sibling = (group, my_z, my_t + 1 - 2 * core)

    after = [lax.rem(me + step, experts) for step in range(experts)]
    holder = [
        (group, lax.div(number, pairs), lax.rem(number, pairs) * 2 + core) for number in after
    ]
    tensor_after = [lax.rem(my_t + step, tensor_ranks) for step in range(tensor_ranks)]

    small = [
        pltpu.make_async_copy(source, target, in_sem.at[i])
        for i, (source, target) in enumerate(
            (
                (attn_hbm, attn),
                (resid_hbm, resid),
                (gain_hbm, gain),
                (router_hbm, router),
                (routes_hbm, routes),
            )
        )
    ]
    for copy in small:
        copy.start()

    barrier = pltpu.get_barrier_semaphore()
    tensor_peers = [(group, my_z, tensor_after[i]) for i in range(1, tensor_ranks, 2)]
    peers = holder[1:]
    for peer in tensor_peers + peers:
        pl.semaphore_signal(barrier, inc=1, device_id=peer, device_id_type=MESH)

    def hidden_copies(step, slot):
        inputs = pl.ds(step * hidden_step, hidden_step)
        return [
            pltpu.make_async_copy(
                source.at[inputs], hidden_weights.at[slot, i], hidden_sem.at[slot, i]
            )
            for i, source in enumerate((gate_hbm, up_hbm))
        ]

    def down_copy(step, slot):
        columns = pl.ds(pl.multiple_of(step * down_step, down_step), down_step)
        return pltpu.make_async_copy(
            down_hbm.at[:, columns], down_weights.at[slot], down_sem.at[slot]
        )

    def start_hidden(step):
        for copy in hidden_copies(step, step):
            copy.start()

    start_hidden(0)
    small[0].wait()
    terms = attn[...].astype(jnp.float32)
    half = features // 2
    for i in range(tensor_ranks):
        block = terms[i * rows : (i + 1) * rows]
        attn_out[i] = jnp.concatenate([block[:, :half], block[:, half:]], axis=0).astype(
            jnp.bfloat16
        )
    pl.semaphore_wait(barrier, len(tensor_peers) + len(peers))

    def attn_copy(step):
        target = tensor_after[step]
        return pltpu.make_async_remote_copy(
            src_ref=attn_out.at[target],
            dst_ref=attn_in.at[step - 1],
            send_sem=attn_out_sem.at[step - 1],
            recv_sem=attn_in_sem.at[step - 1],
            device_id=(group, my_z, target),
            device_id_type=MESH,
        )

    attn_copies = [attn_copy(step) for step in range(1, tensor_ranks)]
    for copy in attn_copies:
        copy.start()
    for step in range(1, min(2, hidden_slots)):
        start_hidden(step)
    for copy in small[1:]:
        copy.wait()
    diagonal = lax.broadcasted_iota(jnp.int32, (rows, rows), 0) == lax.broadcasted_iota(
        jnp.int32, (rows, rows), 1
    )
    first, second = [
        jnp.sum(jnp.where(diagonal, routes[i : i + 1].astype(jnp.float32), 0.0), axis=1, keepdims=True)
        .astype(jnp.int32)
        for i in range(2)
    ]
    columns = lax.broadcasted_iota(jnp.int32, (rows, LANES), 1)
    row_number = lax.broadcasted_iota(jnp.int32, (rows, LANES), 0)
    pick_first = (columns == first).astype(jnp.float32)
    pick_second = (columns == second).astype(jnp.float32)
    both = pick_first + pick_second
    earlier = jnp.zeros((rows, LANES), jnp.float32)
    for i in range(rows):
        earlier += jnp.where(row_number > i, both[i : i + 1], 0.0)
    slot_first = jnp.sum(earlier * pick_first, axis=1, keepdims=True).astype(jnp.int32)
    slot_second = jnp.sum(earlier * pick_second, axis=1, keepdims=True).astype(jnp.int32)
    place_first = jnp.concatenate([first * PACKED_ROWS + slot_first] * fold, axis=0)
    place_second = jnp.concatenate([second * PACKED_ROWS + slot_second] * fold, axis=0)
    packed = experts * PACKED_ROWS
    part = lax.broadcasted_iota(jnp.int32, (fold * rows, packed), 0)
    part = (part >> log(rows)) * capacity
    cells = lax.broadcasted_iota(jnp.int32, (fold * rows, packed), 1) - part
    cell_first = (cells == place_first).astype(jnp.float32)
    cell_second = (cells == place_second).astype(jnp.float32)
    placement = (cell_first + cell_second).T.astype(jnp.bfloat16)

    summed = attn_out[my_t].astype(jnp.float32)
    for i, copy in enumerate(attn_copies):
        copy.wait_recv()
        summed += attn_in[i].astype(jnp.float32)
    attn_sum = jnp.concatenate([summed[:rows], summed[rows:]], axis=1)
    hidden_wide = (
        (resid[...].astype(jnp.float32) + attn_sum).astype(jnp.bfloat16).astype(jnp.float32)
    )
    hidden_ref[...] = hidden_wide
    mean_square = jnp.sum(hidden_wide * hidden_wide, axis=1, keepdims=True) / features
    normed_wide = hidden_wide * lax.rsqrt(mean_square + EPSILON) * gain[...]
    normed = normed_wide.astype(jnp.bfloat16)

    def slot_copy(part, step):
        return pltpu.make_async_remote_copy(
            src_ref=slots_out.at[part, after[step]],
            dst_ref=slots_in.at[part, core, me],
            send_sem=slots_out_sem.at[part],
            recv_sem=slots_in_sem.at[part],
            device_id=holder[step],
            device_id_type=MESH,
        )

    others = pl.ds(0, experts - 1)

    def all_slots(part):
        return pltpu.make_async_remote_copy(
            src_ref=slots_out.at[part, others],
            dst_ref=slots_in.at[part, core, others],
            send_sem=slots_out_sem.at[part],
            recv_sem=slots_in_sem.at[part],
            device_id=sibling,
            device_id_type=MESH,
        )

    def pass_copy(part):
        return pltpu.make_async_remote_copy(
            src_ref=slots_in.at[part, core],
            dst_ref=slots_in.at[part, core],
            send_sem=pass_out_sem.at[part],
            recv_sem=pass_in_sem.at[part],
            device_id=sibling,
            device_id_type=MESH,
        )

    for part in range(parts):
        start = part * part_features
        folded = jnp.concatenate(
            [
                normed_wide[:, start + i * width : start + (i + 1) * width]
                for i in range(fold)
            ],
            axis=0,
        ).astype(jnp.bfloat16)
        outgoing = jnp.dot(placement, folded, preferred_element_type=jnp.float32)
        slots_out[part] = outgoing.astype(jnp.bfloat16).reshape(experts, PACKED_ROWS, width)
        for step in sorted(range(1, experts), key=lambda step: abs(2 * step - experts - 1)):
            slot_copy(part, step).start()
        slots_in[part, core, me] = slots_out[part, me]
    for step in range(2, hidden_slots):
        start_hidden(step)
    for step in range(down_slots):
        down_copy(step, step).start()

    logits = lax.dot_general(
        normed, router[...], (((1,), (1,)), ((), ())), preferred_element_type=jnp.float32
    )
    expert_columns = lax.broadcasted_iota(jnp.int32, (rows, experts), 1)
    logit_first = jnp.sum(jnp.where(expert_columns == first, logits, 0.0), axis=1, keepdims=True)
    logit_second = jnp.sum(jnp.where(expert_columns == second, logits, 0.0), axis=1, keepdims=True)
    share_first = 1.0 / (1.0 + jnp.exp(logit_second - logit_first))
    share_second = 1.0 - share_first
    share = (
        jnp.concatenate([share_first] * fold, axis=0) * cell_first
        + jnp.concatenate([share_second] * fold, axis=0) * cell_second
    )
    for i in range(3):
        term = share.astype(jnp.bfloat16)
        share_ref[i * fold * rows : (i + 1) * fold * rows] = term
        share = share - term.astype(jnp.float32)

    sources = 2 * experts
    token_rows = sources * capacity
    token_number = lax.broadcasted_iota(jnp.int32, (token_rows, sources * PACKED_ROWS), 0)
    packed_number = lax.broadcasted_iota(jnp.int32, (token_rows, sources * PACKED_ROWS), 1)
    wanted = (token_number >> log(capacity)) * PACKED_ROWS + (token_number & (capacity - 1))
    for i in range(fold):
        select[i] = (
            (packed_number == wanted + i * capacity).astype(jnp.float32).astype(jnp.bfloat16)
        )
    half_rows = experts * capacity
    to_row = lax.broadcasted_iota(jnp.int32, (packed, packed), 0)
    from_row = lax.broadcasted_iota(jnp.int32, (packed, packed), 1)
    origin = (
        ((to_row & (PACKED_ROWS - 1)) >> log(capacity)) * half_rows
        + (to_row >> log(PACKED_ROWS)) * capacity
        + (to_row & (capacity - 1))
    )
    reorder[...] = (from_row == origin).astype(jnp.float32).astype(jnp.bfloat16)

    def receive(part):
        all_slots(part).wait_recv()
        pass_copy(part).start()
        pass_copy(part).wait_recv()
        arrived = slots_in[part].reshape(sources * PACKED_ROWS, width)
        for i in range(fold):
            place, column = divmod(i * width, hidden_step)
            tokens[part * part_steps + place, :, column : column + width] = jnp.dot(
                select[i], arrived, preferred_element_type=jnp.float32
            ).astype(jnp.bfloat16)

    tile = fold * LANES
    for step in range(hidden_steps):
        slot = step % hidden_slots
        if step % part_steps == 0:
            receive(step // part_steps)
        for copy in hidden_copies(step, slot):
            copy.wait()
        for start in range(0, hidden_units, tile):
            where = slice(start, start + tile)
            values = []
            for i, total in enumerate((gate_sum, up_sum)):
                value = jnp.dot(
                    tokens[step],
                    hidden_weights[slot, i, :, where],
                    preferred_element_type=jnp.float32,
                )
                values.append(value if step == 0 else total[:, where] + value)
            if step < hidden_steps - 1:
                gate_sum[:, where], up_sum[:, where] = values
            else:
                gate_value, up_value = values
                value = gate_value / (1.0 + jnp.exp(-gate_value)) * up_value
                activated[:, where] = value.astype(jnp.bfloat16)
        if step + hidden_slots < hidden_steps:
            for copy in hidden_copies(step + hidden_slots, slot):
                copy.start()

    def half_copy(step):
        return pltpu.make_async_remote_copy(
            src_ref=half_out.at[step],
            dst_ref=half_in.at[step],
            send_sem=half_out_sem.at[step],
            recv_sem=half_in_sem.at[step],
            device_id=sibling,
            device_id_type=MESH,
        )

    def back_copy(step, distance):
        return pltpu.make_async_remote_copy(
            src_ref=back_out.at[step, after[distance]],
            dst_ref=back_in.at[step, me],
            send_sem=back_out_sem.at[step],
            recv_sem=back_in_sem.at[step],
            device_id=holder[distance],
            device_id_type=MESH,
        )

    def all_back(step):
        return pltpu.make_async_remote_copy(
            src_ref=back_out.at[step, others],
            dst_ref=back_in.at[step, others],
            send_sem=back_out_sem.at[step],
            recv_sem=back_in_sem.at[step],
            device_id=sibling,
            device_id_type=MESH,
        )

    def send_back(step):
        half_copy(step).wait_recv()
        total = partial_ref[step, core] + half_in[step].astype(jnp.float32)
        stacked = jnp.concatenate(
            [total[:, i * span : (i + 1) * span] for i in range(fold)], axis=0
        ).astype(jnp.bfloat16)
        ordered = jnp.dot(reorder[...], stacked, preferred_element_type=jnp.float32)
        back_out[step] = ordered.astype(jnp.bfloat16).reshape(experts, PACKED_ROWS, span)
        for distance in range(1, experts):
            back_copy(step, distance).start()
        back_in[step, me] = back_out[step, me]

    def down_body(step, carry):
        for i in range(chunk_steps):
            piece = step * chunk_steps + i
            slot = piece % down_slots
            down_copy(piece, slot).wait()
            produced = jnp.dot(
                activated[...], down_weights[slot], preferred_element_type=jnp.float32
            )
            partial_ref[step, :, :, i * down_step : (i + 1) * down_step] = produced.reshape(
                2, half_rows, down_step
            )

            @pl.when(piece + down_slots < down_steps)
            def _():
                down_copy(piece + down_slots, slot).start()

            if i == 0:

                @pl.when(step > 0)
                def _():
                    send_back(step - 1)

        half_out[step] = partial_ref[step, 1 - core].astype(jnp.bfloat16)
        half_copy(step).start()
        return carry

    lax.fori_loop(0, chunks, down_body, 0)

    def combine(step):
        all_back(step).wait_recv()
        mixed = jnp.dot(
            share_ref[...],
            back_in[step].reshape(packed, span),
            preferred_element_type=jnp.float32,
        )
        terms = fold * rows
        mixed = mixed[:terms] + (mixed[terms : 2 * terms] + mixed[2 * terms :])
        for i in range(fold):
            where = slice(step * chunk + i * span, step * chunk + (i + 1) * span)
            out_ref[:, where] = (
                hidden_ref[:, where] + mixed[i * rows : (i + 1) * rows]
            ).astype(jnp.bfloat16)

    for step in range(chunks - 2):
        combine(step)
    send_back(chunks - 1)
    for step in range(max(0, chunks - 2), chunks):
        combine(step)

    for copy in attn_copies:
        copy.wait_send()
    for part in range(parts):
        all_slots(part).wait_send()
        pass_copy(part).wait_send()
    for step in range(chunks):
        half_copy(step).wait_send()
        all_back(step).wait_send()


def fused_shards(resid, attn_part, norm_gain, w_router, routes, w_gate, w_up, w_down):
    tensor_ranks = lax.axis_size("tensor")
    rows, features = resid.shape
    capacity = rows // 2
    fold = PACKED_ROWS // capacity
    hidden_units = w_gate.shape[1]
    parts = 2
    width = features // parts // fold
    step = fold * LANES
    hidden_step = 2 * width
    hidden_steps, down_steps = features // hidden_step, features // step
    down_slots = min(down_steps, 4)
    chunk = 2 * step if down_steps % 2 == 0 else step
    chunks = features // chunk
    hidden_bytes, down_bytes = 4 * hidden_units * hidden_step, 2 * hidden_units * step
    hidden_slots = min(hidden_steps, (WEIGHT_BYTES - down_slots * down_bytes) // hidden_bytes)
    dma = pltpu.SemaphoreType.DMA
    bf16, f32 = jnp.bfloat16, jnp.float32
    half_rows = E * capacity
    weights = 2 * features * hidden_units + hidden_units * features
    return pl.pallas_call(
        functools.partial(fused_kernel, (E, tensor_ranks, capacity, hidden_slots, down_slots)),
        out_shape=jax.ShapeDtypeStruct(resid.shape, bf16),
        in_specs=[pl.BlockSpec(memory_space=pl.ANY)] * 8,
        out_specs=pl.BlockSpec(memory_space=pltpu.VMEM),
        scratch_shapes=[
            pltpu.VMEM(resid.shape, bf16),
            pltpu.VMEM(attn_part.shape, bf16),
            pltpu.VMEM((1, features), f32),
            pltpu.VMEM(w_router.shape[::-1], bf16),
            pltpu.VMEM(routes.shape[::-1], jnp.int32),
            dma((5,)),
            pltpu.VMEM((hidden_slots, 2, hidden_step, hidden_units), bf16),
            dma((hidden_slots, 2)),
            pltpu.VMEM((down_slots, hidden_units, step), bf16),
            dma((down_slots,)),
            pltpu.VMEM((tensor_ranks, 2 * rows, features // 2), bf16),
            pltpu.VMEM((tensor_ranks - 1, 2 * rows, features // 2), bf16),
            dma((tensor_ranks - 1,)),
            dma((tensor_ranks - 1,)),
            pltpu.VMEM(resid.shape, f32),
            pltpu.VMEM((3 * fold * rows, E * PACKED_ROWS), bf16),
            pltpu.VMEM((parts, E, PACKED_ROWS, width), bf16),
            pltpu.VMEM((parts, 2, E, PACKED_ROWS, width), bf16),
            dma((parts,)),
            dma((parts,)),
            dma((parts,)),
            dma((parts,)),
            pltpu.VMEM((fold, 2 * half_rows, 2 * E * PACKED_ROWS), bf16),
            pltpu.VMEM((E * PACKED_ROWS, E * PACKED_ROWS), bf16),
            pltpu.VMEM((hidden_steps, 2 * half_rows, hidden_step), bf16),
            pltpu.VMEM((2 * half_rows, hidden_units), f32),
            pltpu.VMEM((2 * half_rows, hidden_units), f32),
            pltpu.VMEM((2 * half_rows, hidden_units), bf16),
            pltpu.VMEM((chunks, 2, half_rows, chunk), f32),
            pltpu.VMEM((chunks, half_rows, chunk), bf16),
            pltpu.VMEM((chunks, half_rows, chunk), bf16),
            dma((chunks,)),
            dma((chunks,)),
            pltpu.VMEM((chunks, E, PACKED_ROWS, chunk // fold), bf16),
            pltpu.VMEM((chunks, E, PACKED_ROWS, chunk // fold), bf16),
            dma((chunks,)),
            dma((chunks,)),
        ],
        compiler_params=pltpu.CompilerParams(
            collective_id=0, has_side_effects=True, vmem_limit_bytes=VMEM_BYTES
        ),
        cost_estimate=pl.CostEstimate(
            flops=2 * 2 * half_rows * weights,
            bytes_accessed=2 * weights,
            transcendentals=2 * half_rows * hidden_units,
        ),
    )(resid, attn_part, norm_gain.reshape(1, features), w_router.T, routes.T, w_gate, w_up, w_down)


def fits(mesh):
    ranks = mesh.shape["expert"] * mesh.shape["tensor"]
    return ranks == 2 * E and mesh.shape["tensor"] % 2 == 0


def solution(mesh):
    return jax.shard_map(
        fused_shards if fits(mesh) else shards,
        mesh=mesh,
        in_specs=(
            P(("groups", "expert", "tensor"), None),
            P(("groups", "expert"), "tensor"),
            P(),
            P(),
            P(("groups", "expert", "tensor"), None),
            P(None, ("expert", "tensor")),
            P(None, ("expert", "tensor")),
            P(("expert", "tensor"), None),
        ),
        out_specs=P(("groups", "expert", "tensor"), None),
        check_vma=False,
    )
```

```python
import functools

import jax
import jax.numpy as jnp
from jax import lax
from jax.experimental import pallas as pl
from jax.experimental.pallas import tpu as pltpu
from jax.sharding import PartitionSpec as P

E = 8
MESH = pl.DeviceIdType.MESH


EPSILON = 1e-05


def partner(shard, axis, distance):
    return lax.ppermute(shard, axis, [(i, i ^ 1 << distance) for i in range(lax.axis_size(axis))])


def shards(resid, attn_part, norm_gain, w_router, routes, w_gate, w_up, w_down):
    expert_ranks = lax.axis_size("expert")
    tensor_ranks = lax.axis_size("tensor")
    my_expert_rank = lax.axis_index("expert")
    my_tensor_rank = lax.axis_index("tensor")
    token_rows = resid.shape[0]
    feature_count = resid.shape[1]
    holders = max(1, expert_ranks // E)
    hosted = max(1, E // expert_ranks)
    expert_groups = E // hosted
    capacity = token_rows // 2
    rank_slots = hosted * capacity
    feature_share = feature_count // holders
    levels = holders.bit_length() - 1
    partial_terms = attn_part.astype(jnp.float32)
    attn_rows = lax.psum_scatter(
        partial_terms.astype(jnp.bfloat16), "tensor", scatter_dimension=0, tiled=True
    ).astype(jnp.float32)
    hidden_state = (resid.astype(jnp.float32) + attn_rows).astype(jnp.bfloat16)
    hidden_wide = lax.optimization_barrier(hidden_state).astype(jnp.float32)
    inverse_rms = lax.rsqrt(jnp.mean(hidden_wide * hidden_wide, axis=1, keepdims=True) + EPSILON)
    normed = (hidden_wide * inverse_rms * norm_gain).astype(jnp.bfloat16)
    logits = jnp.dot(normed, w_router, preferred_element_type=jnp.float32)
    expert_columns = lax.broadcasted_iota(jnp.int32, (token_rows, E), 1)
    pick_first = (routes[:, 0:1] == expert_columns).astype(jnp.float32)
    pick_second = (routes[:, 1:2] == expert_columns).astype(jnp.float32)
    share_first = jax.nn.sigmoid(jnp.sum((pick_first - pick_second) * logits, axis=1))
    share_second = 1.0 - share_first
    row_later = lax.broadcasted_iota(jnp.int32, (token_rows, token_rows), 0)
    row_earlier = lax.broadcasted_iota(jnp.int32, (token_rows, token_rows), 1)
    earlier = (row_later > row_earlier).astype(jnp.float32)
    before = jnp.dot(earlier, pick_first + pick_second, precision=lax.Precision.HIGHEST)
    slot_first = jnp.sum(before * pick_first, axis=1)
    slot_second = jnp.sum(before * pick_second, axis=1)
    slot_numbers = lax.broadcasted_iota(jnp.int32, (token_rows, E, capacity), 2).astype(jnp.float32)
    cell_first = pick_first[:, :, None] * (slot_numbers == slot_first[:, None, None]).astype(
        jnp.float32
    )
    cell_second = pick_second[:, :, None] * (slot_numbers == slot_second[:, None, None]).astype(
        jnp.float32
    )
    placement = (
        (cell_first + cell_second)
        .reshape(token_rows, expert_groups, rank_slots)
        .astype(jnp.bfloat16)
    )
    combine_weight = (
        share_first[:, None, None] * cell_first + share_second[:, None, None] * cell_second
    ).reshape(token_rows, expert_groups, rank_slots)
    outgoing = jnp.einsum(
        "rgc,rd->gcd", placement, normed, preferred_element_type=jnp.float32
    ).astype(jnp.bfloat16)
    outgoing = jnp.repeat(outgoing, holders, axis=0)
    arrived = lax.all_to_all(outgoing, "expert", split_axis=0, concat_axis=0, tiled=True)
    device_span = my_expert_rank * tensor_ranks + my_tensor_rank
    own_expert = device_span * E // (expert_ranks * tensor_ranks)
    local_index = own_expert - my_expert_rank // holders * hosted

    def activate(token_block):
        source_count = token_block.shape[0]
        selected = lax.dynamic_slice_in_dim(token_block, local_index * capacity, capacity, 1)
        flattened = selected.reshape(source_count * capacity, feature_count)
        gate_value = jnp.dot(flattened, w_gate, preferred_element_type=jnp.float32)
        up_value = jnp.dot(flattened, w_up, preferred_element_type=jnp.float32)
        return (jax.nn.silu(gate_value) * up_value).astype(jnp.bfloat16)

    def expert_partial(token_block):
        source_count = token_block.shape[0]
        activated = activate(token_block)
        produced = jnp.dot(activated, w_down, preferred_element_type=jnp.float32).reshape(
            source_count, capacity, feature_count
        )
        if hosted == 1:
            return produced
        blank = jnp.zeros((source_count, rank_slots, feature_count), jnp.float32)
        return lax.dynamic_update_slice_in_dim(blank, produced, local_index * capacity, 1)

    partial_value = expert_partial(lax.all_gather(arrived, "tensor", axis=0, tiled=True))
    leading = partial_value.shape[0]
    layered = partial_value.reshape((leading, rank_slots) + (2,) * levels + (feature_share,))
    remaining = [section for section in range(levels - 1, -1, -1)]
    for section in range(levels):
        split_axis = 2 + remaining.index(section)
        my_side = my_expert_rank // 2**section % 2
        kept_half = lax.dynamic_index_in_dim(layered, my_side, split_axis, keepdims=False)
        given_half = lax.dynamic_index_in_dim(layered, 1 - my_side, split_axis, keepdims=False)
        layered = kept_half + partner(given_half.astype(jnp.bfloat16), "expert", section).astype(
            given_half.dtype
        )
        remaining = [other for other in remaining if other != section]
    own_sources = lax.psum_scatter(
        layered.astype(jnp.bfloat16), "tensor", scatter_dimension=0, tiled=True
    ).astype(jnp.float32)
    returned = lax.all_to_all(
        own_sources.astype(jnp.bfloat16), "expert", split_axis=0, concat_axis=0, tiled=True
    ).astype(own_sources.dtype)
    returned_view = returned.reshape(expert_groups, holders, rank_slots, feature_share)
    mixed = jnp.einsum(
        "rgc,gscp->rsp", combine_weight, returned_view, precision=lax.Precision.HIGHEST
    )
    mixed = mixed.reshape(token_rows, feature_count)
    return (hidden_wide + mixed).astype(jnp.bfloat16)


LANES = 128
PACKED_ROWS = 16
WEIGHT_BYTES = 52 << 20
VMEM_BYTES = 61 << 20


def log(power):
    return power.bit_length() - 1


def fused_kernel(
    sizes,
    resid_hbm,
    attn_hbm,
    gain_hbm,
    router_hbm,
    routes_hbm,
    gate_hbm,
    up_hbm,
    down_hbm,
    out_ref,
    resid,
    attn,
    gain,
    router,
    routes,
    in_sem,
    hidden_weights,
    hidden_sem,
    down_weights,
    down_sem,
    attn_out,
    attn_in,
    attn_out_sem,
    attn_in_sem,
    hidden_ref,
    share_ref,
    slots_out,
    slots_in,
    slots_out_sem,
    slots_in_sem,
    pass_out_sem,
    pass_in_sem,
    select,
    reorder,
    tokens,
    gate_sum,
    up_sum,
    activated,
    partial_ref,
    half_out,
    half_in,
    half_out_sem,
    half_in_sem,
    back_out,
    back_in,
    back_out_sem,
    back_in_sem,
):
    experts, tensor_ranks, capacity, hidden_slots, down_slots = sizes
    rows, features = resid.shape
    fold = PACKED_ROWS // capacity
    parts = slots_out.shape[0]
    part_features = features // parts
    width = part_features // fold
    hidden_units = gate_hbm.shape[1]
    hidden_step = hidden_weights.shape[2]
    hidden_steps = features // hidden_step
    part_steps = hidden_steps // parts
    down_step = down_weights.shape[2]
    chunks, _, _, chunk = partial_ref.shape
    chunk_steps = chunk // down_step
    down_steps = chunks * chunk_steps
    span = chunk // fold
    pairs = tensor_ranks // 2
    group = lax.axis_index("groups")
    my_z = lax.axis_index("expert")
    my_t = lax.axis_index("tensor")
    core = lax.rem(my_t, 2)
    me = my_z * pairs + lax.div(my_t, 2)
    sibling = (group, my_z, my_t + 1 - 2 * core)

    after = [lax.rem(me + step, experts) for step in range(experts)]
    holder = [
        (group, lax.div(number, pairs), lax.rem(number, pairs) * 2 + core) for number in after
    ]
    tensor_after = [lax.rem(my_t + step, tensor_ranks) for step in range(tensor_ranks)]

    small = [
        pltpu.make_async_copy(source, target, in_sem.at[i])
        for i, (source, target) in enumerate(
            (
                (attn_hbm, attn),
                (resid_hbm, resid),
                (gain_hbm, gain),
                (router_hbm, router),
                (routes_hbm, routes),
            )
        )
    ]
    for copy in small:
        copy.start()

    barrier = pltpu.get_barrier_semaphore()
    tensor_peers = [(group, my_z, tensor_after[i]) for i in range(1, tensor_ranks, 2)]
    peers = holder[1:]
    for peer in tensor_peers + peers:
        pl.semaphore_signal(barrier, inc=1, device_id=peer, device_id_type=MESH)

    def hidden_copies(step, slot):
        inputs = pl.ds(step * hidden_step, hidden_step)
        return [
            pltpu.make_async_copy(
                source.at[inputs], hidden_weights.at[slot, i], hidden_sem.at[slot, i]
            )
            for i, source in enumerate((gate_hbm, up_hbm))
        ]

    def down_copy(step, slot):
        columns = pl.ds(pl.multiple_of(step * down_step, down_step), down_step)
        return pltpu.make_async_copy(
            down_hbm.at[:, columns], down_weights.at[slot], down_sem.at[slot]
        )

    def start_hidden(step):
        for copy in hidden_copies(step, step):
            copy.start()

    for step in range(hidden_slots):
        start_hidden(step)
    small[0].wait()
    terms = attn[...].astype(jnp.float32)
    half = features // 2
    for i in range(tensor_ranks):
        block = terms[i * rows : (i + 1) * rows]
        attn_out[i] = jnp.concatenate([block[:, :half], block[:, half:]], axis=0).astype(
            jnp.bfloat16
        )
    pl.semaphore_wait(barrier, len(tensor_peers) + len(peers))

    def attn_copy(step):
        target = tensor_after[step]
        return pltpu.make_async_remote_copy(
            src_ref=attn_out.at[target],
            dst_ref=attn_in.at[step - 1],
            send_sem=attn_out_sem.at[step - 1],
            recv_sem=attn_in_sem.at[step - 1],
            device_id=(group, my_z, target),
            device_id_type=MESH,
        )

    attn_copies = [attn_copy(step) for step in range(1, tensor_ranks)]
    for copy in attn_copies:
        copy.start()
    for copy in small[1:]:
        copy.wait()
    diagonal = lax.broadcasted_iota(jnp.int32, (rows, rows), 0) == lax.broadcasted_iota(
        jnp.int32, (rows, rows), 1
    )
    first, second = [
        jnp.sum(jnp.where(diagonal, routes[i : i + 1].astype(jnp.float32), 0.0), axis=1, keepdims=True)
        .astype(jnp.int32)
        for i in range(2)
    ]
    columns = lax.broadcasted_iota(jnp.int32, (rows, LANES), 1)
    row_number = lax.broadcasted_iota(jnp.int32, (rows, LANES), 0)
    pick_first = (columns == first).astype(jnp.float32)
    pick_second = (columns == second).astype(jnp.float32)
    both = pick_first + pick_second
    earlier = jnp.zeros((rows, LANES), jnp.float32)
    for i in range(rows):
        earlier += jnp.where(row_number > i, both[i : i + 1], 0.0)
    slot_first = jnp.sum(earlier * pick_first, axis=1, keepdims=True).astype(jnp.int32)
    slot_second = jnp.sum(earlier * pick_second, axis=1, keepdims=True).astype(jnp.int32)
    place_first = jnp.concatenate([first * PACKED_ROWS + slot_first] * fold, axis=0)
    place_second = jnp.concatenate([second * PACKED_ROWS + slot_second] * fold, axis=0)
    packed = experts * PACKED_ROWS
    part = lax.broadcasted_iota(jnp.int32, (fold * rows, packed), 0)
    part = (part >> log(rows)) * capacity
    cells = lax.broadcasted_iota(jnp.int32, (fold * rows, packed), 1) - part
    cell_first = (cells == place_first).astype(jnp.float32)
    cell_second = (cells == place_second).astype(jnp.float32)
    placement = (cell_first + cell_second).T.astype(jnp.bfloat16)

    summed = attn_out[my_t].astype(jnp.float32)
    for i, copy in enumerate(attn_copies):
        copy.wait_recv()
        summed += attn_in[i].astype(jnp.float32)
    attn_sum = jnp.concatenate([summed[:rows], summed[rows:]], axis=1)
    hidden_wide = (
        (resid[...].astype(jnp.float32) + attn_sum).astype(jnp.bfloat16).astype(jnp.float32)
    )
    hidden_ref[...] = hidden_wide
    mean_square = jnp.sum(hidden_wide * hidden_wide, axis=1, keepdims=True) / features
    normed_wide = hidden_wide * lax.rsqrt(mean_square + EPSILON) * gain[...]
    normed = normed_wide.astype(jnp.bfloat16)

    def slot_copy(part, step):
        return pltpu.make_async_remote_copy(
            src_ref=slots_out.at[part, after[step]],
            dst_ref=slots_in.at[part, core, me],
            send_sem=slots_out_sem.at[part],
            recv_sem=slots_in_sem.at[part],
            device_id=holder[step],
            device_id_type=MESH,
        )

    others = pl.ds(0, experts - 1)

    def all_slots(part):
        return pltpu.make_async_remote_copy(
            src_ref=slots_out.at[part, others],
            dst_ref=slots_in.at[part, core, others],
            send_sem=slots_out_sem.at[part],
            recv_sem=slots_in_sem.at[part],
            device_id=sibling,
            device_id_type=MESH,
        )

    def pass_copy(part):
        return pltpu.make_async_remote_copy(
            src_ref=slots_in.at[part, core],
            dst_ref=slots_in.at[part, core],
            send_sem=pass_out_sem.at[part],
            recv_sem=pass_in_sem.at[part],
            device_id=sibling,
            device_id_type=MESH,
        )

    for part in range(parts):
        start = part * part_features
        folded = jnp.concatenate(
            [
                normed_wide[:, start + i * width : start + (i + 1) * width]
                for i in range(fold)
            ],
            axis=0,
        ).astype(jnp.bfloat16)
        outgoing = jnp.dot(placement, folded, preferred_element_type=jnp.float32)
        slots_out[part] = outgoing.astype(jnp.bfloat16).reshape(experts, PACKED_ROWS, width)
        for step in sorted(range(1, experts), key=lambda step: abs(2 * step - experts - 1)):
            slot_copy(part, step).start()
        slots_in[part, core, me] = slots_out[part, me]
    for step in range(down_slots):
        down_copy(step, step).start()

    logits = lax.dot_general(
        normed, router[...], (((1,), (1,)), ((), ())), preferred_element_type=jnp.float32
    )
    expert_columns = lax.broadcasted_iota(jnp.int32, (rows, experts), 1)
    logit_first = jnp.sum(jnp.where(expert_columns == first, logits, 0.0), axis=1, keepdims=True)
    logit_second = jnp.sum(jnp.where(expert_columns == second, logits, 0.0), axis=1, keepdims=True)
    share_first = 1.0 / (1.0 + jnp.exp(logit_second - logit_first))
    share_second = 1.0 - share_first
    share = (
        jnp.concatenate([share_first] * fold, axis=0) * cell_first
        + jnp.concatenate([share_second] * fold, axis=0) * cell_second
    )
    for i in range(3):
        term = share.astype(jnp.bfloat16)
        share_ref[i * fold * rows : (i + 1) * fold * rows] = term
        share = share - term.astype(jnp.float32)

    sources = 2 * experts
    token_rows = sources * capacity
    token_number = lax.broadcasted_iota(jnp.int32, (token_rows, sources * PACKED_ROWS), 0)
    packed_number = lax.broadcasted_iota(jnp.int32, (token_rows, sources * PACKED_ROWS), 1)
    wanted = (token_number >> log(capacity)) * PACKED_ROWS + (token_number & (capacity - 1))
    for i in range(fold):
        select[i] = (
            (packed_number == wanted + i * capacity).astype(jnp.float32).astype(jnp.bfloat16)
        )
    half_rows = experts * capacity
    to_row = lax.broadcasted_iota(jnp.int32, (packed, packed), 0)
    from_row = lax.broadcasted_iota(jnp.int32, (packed, packed), 1)
    origin = (
        ((to_row & (PACKED_ROWS - 1)) >> log(capacity)) * half_rows
        + (to_row >> log(PACKED_ROWS)) * capacity
        + (to_row & (capacity - 1))
    )
    reorder[...] = (from_row == origin).astype(jnp.float32).astype(jnp.bfloat16)

    def receive(part):
        all_slots(part).wait_recv()
        pass_copy(part).start()
        pass_copy(part).wait_recv()
        arrived = slots_in[part].reshape(sources * PACKED_ROWS, width)
        for i in range(fold):
            place, column = divmod(i * width, hidden_step)
            tokens[part * part_steps + place, :, column : column + width] = jnp.dot(
                select[i], arrived, preferred_element_type=jnp.float32
            ).astype(jnp.bfloat16)

    tile = fold * LANES
    for step in range(hidden_steps):
        slot = step % hidden_slots
        if step % part_steps == 0:
            receive(step // part_steps)
        for copy in hidden_copies(step, slot):
            copy.wait()
        for start in range(0, hidden_units, tile):
            where = slice(start, start + tile)
            values = []
            for i, total in enumerate((gate_sum, up_sum)):
                value = jnp.dot(
                    tokens[step],
                    hidden_weights[slot, i, :, where],
                    preferred_element_type=jnp.float32,
                )
                values.append(value if step == 0 else total[:, where] + value)
            if step < hidden_steps - 1:
                gate_sum[:, where], up_sum[:, where] = values
            else:
                gate_value, up_value = values
                value = gate_value / (1.0 + jnp.exp(-gate_value)) * up_value
                activated[:, where] = value.astype(jnp.bfloat16)
        if step + hidden_slots < hidden_steps:
            for copy in hidden_copies(step + hidden_slots, slot):
                copy.start()

    def half_copy(step):
        return pltpu.make_async_remote_copy(
            src_ref=half_out.at[step],
            dst_ref=half_in.at[step],
            send_sem=half_out_sem.at[step],
            recv_sem=half_in_sem.at[step],
            device_id=sibling,
            device_id_type=MESH,
        )

    def back_copy(step, distance):
        return pltpu.make_async_remote_copy(
            src_ref=back_out.at[step, after[distance]],
            dst_ref=back_in.at[step, me],
            send_sem=back_out_sem.at[step],
            recv_sem=back_in_sem.at[step],
            device_id=holder[distance],
            device_id_type=MESH,
        )

    def all_back(step):
        return pltpu.make_async_remote_copy(
            src_ref=back_out.at[step, others],
            dst_ref=back_in.at[step, others],
            send_sem=back_out_sem.at[step],
            recv_sem=back_in_sem.at[step],
            device_id=sibling,
            device_id_type=MESH,
        )

    def send_back(step):
        half_copy(step).wait_recv()
        total = partial_ref[step, core] + half_in[step].astype(jnp.float32)
        stacked = jnp.concatenate(
            [total[:, i * span : (i + 1) * span] for i in range(fold)], axis=0
        ).astype(jnp.bfloat16)
        ordered = jnp.dot(reorder[...], stacked, preferred_element_type=jnp.float32)
        back_out[step] = ordered.astype(jnp.bfloat16).reshape(experts, PACKED_ROWS, span)
        for distance in range(1, experts):
            back_copy(step, distance).start()
        back_in[step, me] = back_out[step, me]

    def down_body(step, carry):
        for i in range(chunk_steps):
            piece = step * chunk_steps + i
            slot = piece % down_slots
            down_copy(piece, slot).wait()
            produced = jnp.dot(
                activated[...], down_weights[slot], preferred_element_type=jnp.float32
            )
            partial_ref[step, :, :, i * down_step : (i + 1) * down_step] = produced.reshape(
                2, half_rows, down_step
            )

            @pl.when(piece + down_slots < down_steps)
            def _():
                down_copy(piece + down_slots, slot).start()

            if i == 0:

                @pl.when(step > 0)
                def _():
                    send_back(step - 1)

        half_out[step] = partial_ref[step, 1 - core].astype(jnp.bfloat16)
        half_copy(step).start()
        return carry

    lax.fori_loop(0, chunks, down_body, 0)

    def combine(step):
        all_back(step).wait_recv()
        mixed = jnp.dot(
            share_ref[...],
            back_in[step].reshape(packed, span),
            preferred_element_type=jnp.float32,
        )
        terms = fold * rows
        mixed = mixed[:terms] + (mixed[terms : 2 * terms] + mixed[2 * terms :])
        for i in range(fold):
            where = slice(step * chunk + i * span, step * chunk + (i + 1) * span)
            out_ref[:, where] = (
                hidden_ref[:, where] + mixed[i * rows : (i + 1) * rows]
            ).astype(jnp.bfloat16)

    for step in range(chunks - 2):
        combine(step)
    send_back(chunks - 1)
    for step in range(max(0, chunks - 2), chunks):
        combine(step)

    for copy in attn_copies:
        copy.wait_send()
    for part in range(parts):
        all_slots(part).wait_send()
        pass_copy(part).wait_send()
    for step in range(chunks):
        half_copy(step).wait_send()
        all_back(step).wait_send()


def fused_shards(resid, attn_part, norm_gain, w_router, routes, w_gate, w_up, w_down):
    tensor_ranks = lax.axis_size("tensor")
    rows, features = resid.shape
    capacity = rows // 2
    fold = PACKED_ROWS // capacity
    hidden_units = w_gate.shape[1]
    parts = 2
    width = features // parts // fold
    step = fold * LANES
    hidden_step = 2 * width
    hidden_steps, down_steps = features // hidden_step, features // step
    down_slots = min(down_steps, 4)
    chunk = 2 * step if down_steps % 2 == 0 else step
    chunks = features // chunk
    hidden_bytes, down_bytes = 4 * hidden_units * hidden_step, 2 * hidden_units * step
    hidden_slots = min(hidden_steps, (WEIGHT_BYTES - down_slots * down_bytes) // hidden_bytes)
    dma = pltpu.SemaphoreType.DMA
    bf16, f32 = jnp.bfloat16, jnp.float32
    half_rows = E * capacity
    weights = 2 * features * hidden_units + hidden_units * features
    return pl.pallas_call(
        functools.partial(fused_kernel, (E, tensor_ranks, capacity, hidden_slots, down_slots)),
        out_shape=jax.ShapeDtypeStruct(resid.shape, bf16),
        in_specs=[pl.BlockSpec(memory_space=pl.ANY)] * 8,
        out_specs=pl.BlockSpec(memory_space=pltpu.VMEM),
        scratch_shapes=[
            pltpu.VMEM(resid.shape, bf16),
            pltpu.VMEM(attn_part.shape, bf16),
            pltpu.VMEM((1, features), f32),
            pltpu.VMEM(w_router.shape[::-1], bf16),
            pltpu.VMEM(routes.shape[::-1], jnp.int32),
            dma((5,)),
            pltpu.VMEM((hidden_slots, 2, hidden_step, hidden_units), bf16),
            dma((hidden_slots, 2)),
            pltpu.VMEM((down_slots, hidden_units, step), bf16),
            dma((down_slots,)),
            pltpu.VMEM((tensor_ranks, 2 * rows, features // 2), bf16),
            pltpu.VMEM((tensor_ranks - 1, 2 * rows, features // 2), bf16),
            dma((tensor_ranks - 1,)),
            dma((tensor_ranks - 1,)),
            pltpu.VMEM(resid.shape, f32),
            pltpu.VMEM((3 * fold * rows, E * PACKED_ROWS), bf16),
            pltpu.VMEM((parts, E, PACKED_ROWS, width), bf16),
            pltpu.VMEM((parts, 2, E, PACKED_ROWS, width), bf16),
            dma((parts,)),
            dma((parts,)),
            dma((parts,)),
            dma((parts,)),
            pltpu.VMEM((fold, 2 * half_rows, 2 * E * PACKED_ROWS), bf16),
            pltpu.VMEM((E * PACKED_ROWS, E * PACKED_ROWS), bf16),
            pltpu.VMEM((hidden_steps, 2 * half_rows, hidden_step), bf16),
            pltpu.VMEM((2 * half_rows, hidden_units), f32),
            pltpu.VMEM((2 * half_rows, hidden_units), f32),
            pltpu.VMEM((2 * half_rows, hidden_units), bf16),
            pltpu.VMEM((chunks, 2, half_rows, chunk), f32),
            pltpu.VMEM((chunks, half_rows, chunk), bf16),
            pltpu.VMEM((chunks, half_rows, chunk), bf16),
            dma((chunks,)),
            dma((chunks,)),
            pltpu.VMEM((chunks, E, PACKED_ROWS, chunk // fold), bf16),
            pltpu.VMEM((chunks, E, PACKED_ROWS, chunk // fold), bf16),
            dma((chunks,)),
            dma((chunks,)),
        ],
        compiler_params=pltpu.CompilerParams(
            collective_id=0, has_side_effects=True, vmem_limit_bytes=VMEM_BYTES
        ),
        cost_estimate=pl.CostEstimate(
            flops=2 * 2 * half_rows * weights,
            bytes_accessed=2 * weights,
            transcendentals=2 * half_rows * hidden_units,
        ),
    )(resid, attn_part, norm_gain.reshape(1, features), w_router.T, routes.T, w_gate, w_up, w_down)


def fits(mesh):
    ranks = mesh.shape["expert"] * mesh.shape["tensor"]
    return ranks == 2 * E and mesh.shape["tensor"] % 2 == 0


def solution(mesh):
    return jax.shard_map(
        fused_shards if fits(mesh) else shards,
        mesh=mesh,
        in_specs=(
            P(("groups", "expert", "tensor"), None),
            P(("groups", "expert"), "tensor"),
            P(),
            P(),
            P(("groups", "expert", "tensor"), None),
            P(None, ("expert", "tensor")),
            P(None, ("expert", "tensor")),
            P(("expert", "tensor"), None),
        ),
        out_specs=P(("groups", "expert", "tensor"), None),
        check_vma=False,
    )
```
